32 devices in a mesh: ctx: 8 (over z, x), head: 4 (over y, core).
Axes of the slice: x: 2, y: 2, z: 4, core: 2. Of those that a mesh axis runs over, the one named last changes fastest.
Arguments:
- queries: bfloat16 [512, 64, 128], P('ctx', 'head'), may hold values from -24 to 24
- cache_keys: bfloat16 [2048, 8, 128], P('ctx', 'head'), may hold values from -24 to 24
- cache_values: bfloat16 [2048, 8, 128], P('ctx', 'head'), may hold values from -6 to 6
- new_keys: bfloat16 [512, 8, 128], P('ctx', 'head'), may hold values from -6 to 6
- new_values: bfloat16 [512, 8, 128], P('ctx', 'head'), may hold values from -6 to 6
- frame_of_slot: int32 [8], P('ctx'), may hold values from 0 to 7, each once
- slopes: float32 [64], P('head'), may hold values from 0.002 to 0.1
Outputs:
- attended: bfloat16 [512, 8192], P('ctx')
The draws below stay inside these ranges and needn't reach their ends.
Inputs may be any that keep to these rules, and one draw needn't show every extreme that they name: `frame_of_slot`: each frame number 0 to 7 stands in exactly one slot.
All inputs are finite; a program needn't handle non-finite values.
Results may differ from the reference program's by a relative error of at most 0.0085.
Values may be sent and summed in bfloat16 or wider, within the bound.
A program may use at most 64 MiB of HBM per device.

```python
import math
import jax
import jax.numpy as jnp
from jax import lax

HEADS = 64
KVH = 8
HD = 128
FRAME = 256
QTOK = 512
CACHE_FRAMES = 8
CACHE = 2048


def draw_queries(key, part):
    values = jnp.clip(jax.random.normal(jax.random.fold_in(key, 1), (QTOK, HEADS, HD), jnp.float32), -5.0, 5.0)
    return values.astype(jnp.bfloat16)


def draw_cache_keys(key, part):
    values = jnp.clip(jax.random.normal(jax.random.fold_in(key, 2), (CACHE, KVH, HD), jnp.float32), -5.0, 5.0)
    return values.astype(jnp.bfloat16)


def level_of(rng, dims, pieces, low, high):
    factor_of = 1.0
    for position, blocks in pieces:
        steps = jax.random.uniform(jax.random.fold_in(jax.random.fold_in(rng, 6), position), (blocks,), jnp.float32, low / len(pieces), high / len(pieces))
        factor_of = factor_of * jnp.repeat(jnp.exp(steps), dims[position] // blocks).reshape((-1,) + (1,) * (len(dims) - 1 - position))
    return factor_of


def noise(key, extent, width, reach, split=(), kind=jnp.bfloat16):
    values = width * jax.random.normal(key, extent, jnp.float32)
    if split:
        values = values * level_of(key, extent, split, -0.22, 0.18)
    return jnp.clip(values, -reach, reach).astype(kind)


def setup_inputs(seed: int = 0) -> dict:
    keys = jax.random.split(jax.random.key(seed), 8)
    return {
        "queries": draw_queries(jax.random.fold_in(keys[7], 71), 0),
        "cache_keys": draw_cache_keys(jax.random.fold_in(keys[7], 71), 0),
        "cache_values": noise(keys[2], (CACHE, KVH, HD), 1.0, 6.0, ((0, 8), (1, 4))),
        "new_keys": noise(keys[3], (QTOK, KVH, HD), 1.0, 6.0, ((0, 8), (1, 4))),
        "new_values": noise(keys[4], (QTOK, KVH, HD), 1.0, 6.0, ((0, 8), (1, 4))),
        "frame_of_slot": jax.random.permutation(keys[5], CACHE_FRAMES).astype(jnp.int32),
        "slopes": jnp.clip(jnp.exp(math.log(0.1) - 3.912023 * jax.random.uniform(keys[6], (HEADS,), jnp.float32) ** level_of(keys[6], (HEADS,), ((0, 4),), -0.2, 0.2)), 0.002, 0.1),
    }


def reference(queries, cache_keys, cache_values, new_keys, new_values, frame_of_slot, slopes):
    group = HEADS // KVH
    scale = 1.0 / (HD ** 0.5)
    qpos = jnp.arange(QTOK, dtype=jnp.int32)
    qframe = (CACHE_FRAMES + qpos // FRAME).astype(jnp.float32)
    cframe = jnp.repeat(frame_of_slot, FRAME).astype(jnp.float32)
    nframe = qframe
    block = 8 * FRAME
    blocks = CACHE // block
    qall = jnp.transpose(queries.reshape(QTOK, KVH, group, HD), (1, 0, 2, 3))
    kall = jnp.transpose(cache_keys, (1, 0, 2)).reshape(KVH, blocks, block, HD)
    vall = jnp.transpose(cache_values, (1, 0, 2)).reshape(KVH, blocks, block, HD)
    knew = jnp.transpose(new_keys, (1, 0, 2))
    vnew = jnp.transpose(new_values, (1, 0, 2))
    slope_all = slopes.reshape(KVH, group)
    cframe_blocks = cframe.reshape(blocks, block)
    causal = qpos[None, :] <= qpos[:, None]

    def update(state, score, values):
        acc, high, total = state
        new_high = jnp.maximum(high, jnp.max(score, axis=-1))
        corr = jnp.exp(high - new_high)
        expo = jnp.exp(score - new_high[..., None])
        total = total * corr + jnp.sum(expo, axis=-1)
        weight = lax.optimization_barrier(expo.astype(jnp.bfloat16)).astype(jnp.float32)
        acc = acc * corr[..., None] + jnp.einsum("tqk,kd->tqd", weight, values.astype(jnp.float32))
        return acc, new_high, total

    def one_group(items):
        qg, kg, vg, kn, vn, sl = items
        q32 = qg.astype(jnp.float32)
        init = (jnp.zeros((QTOK, group, HD), jnp.float32), jnp.full((QTOK, group), -1e30, jnp.float32), jnp.zeros((QTOK, group), jnp.float32))

        def scan_step(state, xs):
            kb, vb, fb = xs
            score = jnp.einsum("tqd,kd->tqk", q32, kb.astype(jnp.float32)) * scale
            score = score - sl[None, :, None] * (qframe[:, None, None] - fb[None, None, :])
            return update(state, score, vb), None

        state, _ = lax.scan(scan_step, init, (kg, vg, cframe_blocks))
        score = jnp.einsum("tqd,kd->tqk", q32, kn.astype(jnp.float32)) * scale
        score = score - sl[None, :, None] * (qframe[:, None, None] - nframe[None, None, :])
        score = jnp.where(causal[:, None, :], score, -1e30)
        acc, high, total = update(state, score, vn)
        return acc / total[..., None]

    outs = lax.map(one_group, (qall, kall, vall, knew, vnew, slope_all))
    return jnp.transpose(outs, (1, 0, 2, 3)).reshape(QTOK, HEADS * HD).astype(jnp.bfloat16)
```

```python
import functools
import math

import jax
import jax.numpy as jnp
from jax import lax
from jax.experimental import pallas as pl
from jax.experimental.pallas import tpu as pltpu
from jax.sharding import PartitionSpec as P

FRAME = 256
MESH = pl.DeviceIdType.MESH
LOG2E = 1.0 / math.log(2.0)
PARTS = 2


def nt(a, b):
    return lax.dot_general(a, b, (((1,), (1,)), ((), ())), preferred_element_type=jnp.float32)


def tn(a, b):
    return lax.dot_general(a, b, (((0,), (0,)), ((), ())), preferred_element_type=jnp.float32)


def iota(shape, dim):
    return lax.broadcasted_iota(jnp.int32, shape, dim)


def kernel(
    sizes,
    q_ref,
    ck_ref,
    cv_ref,
    nk_ref,
    nv_ref,
    frame_ref,
    slope_ref,
    o_ref,
    kv,
    newkv,
    qb,
    acc,
    high,
    total,
    part_out,
    part_in,
    kv_up,
    kv_down,
    kv_recv,
    q_send,
    q_recv,
    p_send,
    p_recv,
    o_send,
    o_recv,
):
    cached, fresh, groups, group, width, shards, heads = sizes
    column = shards // 2
    rows = group * fresh
    cache_frames = shards
    position = lax.axis_index("ctx")
    me = lax.axis_index("head")
    side = position % 2
    place = position // 2
    across = position + 1 - 2 * side
    sibling = me + 1 - 2 * (me % 2)
    peers = [lax.rem(me + 2 * k, heads) for k in range(1, heads // 2)]
    last = column - 1
    has_up = place < last
    has_down = place > 0
    scale = LOG2E / width**0.5
    v_at = cached + fresh
    f_at = 2 * v_at

    barrier = pltpu.get_barrier_semaphore()
    pl.semaphore_signal(barrier, inc=1, device_id={"ctx": across}, device_id_type=MESH)
    for other in [sibling] + peers:
        pl.semaphore_signal(barrier, inc=1, device_id={"head": other}, device_id_type=MESH)

    @pl.when(has_up)
    def _():
        pl.semaphore_signal(barrier, inc=1, device_id={"ctx": position + 2}, device_id_type=MESH)

    @pl.when(has_down)
    def _():
        pl.semaphore_signal(barrier, inc=1, device_id={"ctx": position - 2}, device_id_type=MESH)

    frame = frame_ref[0].astype(jnp.float32)
    for g in range(groups):
        pick = (iota((cached, groups * cached), 1) == groups * iota((cached, groups * cached), 0) + g)
        pick = pick.astype(jnp.float32).astype(jnp.bfloat16)
        few = pick[:fresh, : groups * fresh]
        for src, at, sel, n in (
            (ck_ref, 0, pick, cached),
            (nk_ref, cached, few, fresh),
            (cv_ref, v_at, pick, cached),
            (nv_ref, v_at + cached, few, fresh),
        ):
            kv[place, g, at : at + n, :] = jnp.dot(
                sel, src[...], preferred_element_type=jnp.float32
            ).astype(jnp.bfloat16)
        kv[place, g, f_at : f_at + 16, :] = jnp.full((16, width), frame, jnp.float32).astype(
            jnp.bfloat16
        )

    pl.semaphore_wait(
        barrier, 1 + heads // 2 + jnp.minimum(place, 1) + jnp.minimum(last - place, 1)
    )

    def up(src, g):
        return pltpu.make_async_remote_copy(
            src_ref=kv.at[src, g],
            dst_ref=kv.at[src, g],
            send_sem=kv_up.at[src, g],
            recv_sem=kv_recv.at[src, g],
            device_id={"ctx": position + 2},
            device_id_type=MESH,
        )

    def down(src, g):
        return pltpu.make_async_remote_copy(
            src_ref=kv.at[src, g],
            dst_ref=kv.at[src, g],
            send_sem=kv_down.at[src, g],
            recv_sem=kv_recv.at[src, g],
            device_id={"ctx": position - 2},
            device_id_type=MESH,
        )

    for g in range(groups):

        @pl.when(has_up)
        def _():
            up(place, g).start()

        @pl.when(has_down)
        def _():
            down(place, g).start()

    def q_copy(g):
        return pltpu.make_async_remote_copy(
            src_ref=qb.at[0, g],
            dst_ref=qb.at[1, g],
            send_sem=q_send.at[g],
            recv_sem=q_recv.at[g],
            device_id={"ctx": across},
            device_id_type=MESH,
        )

    local = groups * group
    for g in range(groups):
        r = iota((rows, local * fresh), 0)
        want = (r % fresh) * local + r // fresh + g * group
        pick = (iota((rows, local * fresh), 1) == want).astype(jnp.float32).astype(jnp.bfloat16)
        qb[0, g] = jnp.dot(pick, q_ref[...], preferred_element_type=jnp.float32).astype(jnp.bfloat16)
        q_copy(g).start()

    lane = iota((1, rows), 1)
    token = lane % fresh

    def slope_row(g):
        head = lane // fresh
        row = jnp.zeros((1, rows), jnp.float32)
        for j in range(group):
            row = jnp.where(head == j, slope_ref[g * group + j], row)
        return row * LOG2E

    def query_position(r):
        owner = position if r == 0 else across
        return owner * fresh + token

    def query_frame(r):
        return (cache_frames + query_position(r) // FRAME).astype(jnp.float32)

    for i in range(2 * groups):
        acc[i] = jnp.zeros((width, rows), jnp.float32)
        high[i] = jnp.full((1, rows), -1e30, jnp.float32)
        total[i] = jnp.zeros((1, rows), jnp.float32)

    def update(i, score, shift, values):
        before = high[i]
        now = jnp.maximum(before, jnp.max(score, axis=0, keepdims=True) + shift)
        corr = jnp.exp2(before - now)
        expo = jnp.exp2(score + (shift - now))
        high[i] = now
        total[i] = total[i] * corr + jnp.sum(expo, axis=0, keepdims=True)
        acc[i] = acc[i] * corr + tn(values, expo.astype(jnp.bfloat16))

    def slopes_of(g):
        if isinstance(g, int):
            return slope_row(g)
        row = slope_row(0)
        for k in range(1, groups):
            row = jnp.where(g == k, slope_row(k), row)
        return row

    def attend(src, g):
        keys = kv[src, g, 0:cached, :]
        values = kv[src, g, v_at : v_at + cached, :]
        key_frame = kv[src, g, f_at : f_at + 16, :].astype(jnp.float32)[0:1, 0:1]
        slope = slopes_of(g)
        for r in (1, 0):
            score = nt(keys, qb[r, g]) * scale
            update(2 * g + r, score, -slope * (query_frame(r) - key_frame), values)

    def attend_new(g):
        for src in range(column):
            newkv[0, src * fresh : (src + 1) * fresh, :] = kv[src, g, cached : cached + fresh, :]
            newkv[1, src * fresh : (src + 1) * fresh, :] = kv[
                src, g, v_at + cached : v_at + cached + fresh, :
            ]
        index = iota((column * fresh, 1), 0)
        key_position = ((index // fresh) * 2 + side) * fresh + index % fresh
        key_frame = (cache_frames + key_position // FRAME).astype(jnp.float32)
        slope = slope_row(g)
        for r in (1, 0):
            score = nt(newkv[0], qb[r, g]) * scale - slope * (query_frame(r) - key_frame)
            score = jnp.where(key_position <= query_position(r), score, -1e30)
            update(2 * g + r, score, jnp.zeros((1, rows), jnp.float32), newkv[1])

    def step(apart, g, first):
        low = place - apart
        top = place + apart

        @pl.when(low >= 0)
        def _():
            up(low, g).wait_recv()

            @pl.when(has_up)
            def _():
                up(low, g).start()

        @pl.when(top <= last)
        def _():
            down(top, g).wait_recv()

            @pl.when(has_down)
            def _():
                down(top, g).start()

        @pl.when(first)
        def _():
            q_copy(g).wait_recv()
            attend(place, g)

        @pl.when(low >= 0)
        def _():
            attend(low, g)

        @pl.when(top <= last)
        def _():
            attend(top, g)

    part_rows = rows // PARTS
    part_heads = group // PARTS

    def p_copy(i):
        return pltpu.make_async_remote_copy(
            src_ref=part_out.at[i],
            dst_ref=part_in.at[i],
            send_sem=p_send.at[i],
            recv_sem=p_recv.at[i],
            device_id={"ctx": across},
            device_id_type=MESH,
        )

    def finish(g):
        attend_new(g)
        sub = iota((16, part_rows), 0)
        for c in range(PARTS):
            i = g * PARTS + c
            cols = slice(c * part_rows, (c + 1) * part_rows)
            sums = total[2 * g + 1, :, cols]
            part_out[i, 0:width, :] = (acc[2 * g + 1, :, cols] / sums).astype(jnp.bfloat16)
            lse = high[2 * g + 1, :, cols] + jnp.log(sums) * LOG2E
            one = lse.astype(jnp.bfloat16).astype(jnp.float32)
            two = (lse - one).astype(jnp.bfloat16).astype(jnp.float32)
            three = lse - one - two
            stats = jnp.where(sub == 0, one, jnp.where(sub == 1, two, three))
            part_out[i, width : width + 16, :] = stats.astype(jnp.bfloat16)
            p_copy(i).start()

    def block_of(owner, i):
        at = (owner * groups * PARTS + i) * part_heads * width
        return o_ref.at[:, pl.ds(pl.multiple_of(at, part_heads * width), part_heads * width)]

    def o_copy(owner, i, slot, target):
        return pltpu.make_async_remote_copy(
            src_ref=block_of(owner, i),
            dst_ref=block_of(owner, i),
            send_sem=o_send.at[slot, i],
            recv_sem=o_recv.at[owner, i],
            device_id={"head": target},
            device_id_type=MESH,
        )

    def combine(i):
        g, c = divmod(i, PARTS)
        cols = slice(c * part_rows, (c + 1) * part_rows)
        sums = total[2 * g, :, cols]
        mine = high[2 * g, :, cols] + jnp.log(sums) * LOG2E
        p_copy(i).wait_recv()
        stats = part_in[i, width : width + 16, :].astype(jnp.float32)
        theirs = stats[0:1] + stats[1:2] + stats[2:3]
        top = jnp.maximum(mine, theirs)
        a = jnp.exp2(mine - top)
        b = jnp.exp2(theirs - top)
        both = a + b
        out = acc[2 * g, :, cols] * (a / (sums * both)) + part_in[i, 0:width, :].astype(
            jnp.float32
        ) * (b / both)
        out = out.T
        at = (me * groups * PARTS + i) * part_heads * width
        for j in range(part_heads):
            spot = pl.multiple_of(at + j * width, width)
            o_ref[:, pl.ds(spot, width)] = out[j * fresh : (j + 1) * fresh].astype(jnp.bfloat16)
        for k, peer in enumerate(peers):
            o_copy(me, i, 1 + k, peer).start()
        o_copy(me, i, 0, sibling).start()

    def forward(i):
        for k, peer in enumerate(peers):
            o_copy(peer, i, 0, sibling).wait_recv()
            o_copy(peer, i, 1 + len(peers) + k, sibling).start()

    steps = groups * last

    def body(it, carry):
        apart = it // groups + 1
        step(apart, it % groups, apart == 1)
        return carry

    lax.fori_loop(0, steps - groups + 1, body, 0)
    finish(0)
    for g in range(1, groups):
        step(last, g, last == 1)
        finish(g)

    count = groups * PARTS
    behind = PARTS
    for i in range(count):
        combine(i)
        if i >= behind:
            forward(i - behind)
    for i in range(count - behind, count):
        forward(i)
    for i in range(count):
        o_copy(sibling, i, 0, sibling).wait_recv()
        for peer in peers:
            far = peer + 1 - 2 * (peer % 2)
            o_copy(far, i, 0, sibling).wait_recv()

    for g in range(groups):
        for src in range(column):

            @pl.when(jnp.logical_and(has_up, src <= place))
            def _():
                up(src, g).wait_send()

            @pl.when(jnp.logical_and(has_down, src >= place))
            def _():
                down(src, g).wait_send()

        q_copy(g).wait_send()
    for i in range(count):
        p_copy(i).wait_send()
        o_copy(me, i, 0, sibling).wait_send()
        for k, peer in enumerate(peers):
            o_copy(me, i, 1 + k, peer).wait_send()
            o_copy(peer, i, 1 + len(peers) + k, sibling).wait_send()


def in_one_kernel(queries, cache_keys, cache_values, new_keys, new_values, frame_of_slot, slopes):
    fresh, local, width = queries.shape
    cached, groups, _ = cache_keys.shape
    group = local // groups
    shards = lax.axis_size("ctx")
    heads = lax.axis_size("head")
    column = shards // 2
    rows = group * fresh
    slab = 2 * (cached + fresh) + 16
    count = groups * PARTS
    vmem = pl.BlockSpec(memory_space=pltpu.VMEM)
    smem = pl.BlockSpec(memory_space=pltpu.SMEM)
    dma = pltpu.SemaphoreType.DMA
    sizes = (cached, fresh, groups, group, width, shards, heads)
    return pl.pallas_call(
        functools.partial(kernel, sizes),
        out_shape=jax.ShapeDtypeStruct((fresh, heads * local * width), jnp.bfloat16),
        in_specs=[vmem] * 5 + [smem] * 2,
        out_specs=vmem,
        scratch_shapes=[
            pltpu.VMEM((column, groups, slab, width), jnp.bfloat16),
            pltpu.VMEM((2, column * fresh, width), jnp.bfloat16),
            pltpu.VMEM((2, groups, rows, width), jnp.bfloat16),
            pltpu.VMEM((2 * groups, width, rows), jnp.float32),
            pltpu.VMEM((2 * groups, 1, rows), jnp.float32),
            pltpu.VMEM((2 * groups, 1, rows), jnp.float32),
            pltpu.VMEM((count, width + 16, rows // PARTS), jnp.bfloat16),
            pltpu.VMEM((count, width + 16, rows // PARTS), jnp.bfloat16),
            dma((column, groups)),
            dma((column, groups)),
            dma((column, groups)),
            dma((groups,)),
            dma((groups,)),
            dma((count,)),
            dma((count,)),
            dma((heads - 1, count)),
            dma((heads, count)),
        ],
        compiler_params=pltpu.CompilerParams(
            collective_id=0, has_side_effects=True, vmem_limit_bytes=48 * 1024 * 1024
        ),
        name="attend_over_slice",
    )(
        queries.reshape(fresh * local, width),
        cache_keys.reshape(cached * groups, width),
        cache_values.reshape(cached * groups, width),
        new_keys.reshape(fresh * groups, width),
        new_values.reshape(fresh * groups, width),
        frame_of_slot,
        slopes,
    )


def from_partner(value, axis, apart):
    return lax.ppermute(value, axis, [(i, i ^ 1 << apart) for i in range(lax.axis_size(axis))])


def update(state, score, values):
    acc, high, total = state
    new_high = jnp.maximum(high, jnp.max(score, axis=-1))
    corr = jnp.exp(high - new_high)
    expo = jnp.exp(score - new_high[..., None])
    total = total * corr + jnp.sum(expo, axis=-1)
    weight = expo.astype(jnp.bfloat16)
    acc = acc * corr[..., None] + jnp.einsum(
        "rgqk,kgd->rgqd", weight, values, preferred_element_type=jnp.float32
    )
    return (acc, new_high, total)


def attend(
    q_rows,
    state,
    cache_keys,
    cache_values,
    key_frames,
    new_keys,
    new_values,
    slopes,
    key_start,
    cache_frames,
):
    rows, local_heads, width = q_rows.shape
    groups = cache_keys.shape[1]
    group = local_heads // groups
    scale = 1.0 / width**0.5
    query = q_rows.reshape(rows, groups, group, width)
    qpos = jnp.arange(rows, dtype=jnp.int32)
    qframe = (cache_frames + qpos // FRAME).astype(jnp.float32)
    slope = slopes.reshape(groups, group)
    frames = key_frames.shape[0]
    kblocks = cache_keys.reshape(frames, FRAME, groups, width)
    vblocks = cache_values.reshape(frames, FRAME, groups, width)

    def scan_step(carry, items):
        kb, vb, fb = items
        score = jnp.einsum("rgqd,kgd->rgqk", query, kb, preferred_element_type=jnp.float32) * scale
        distance = qframe - fb.astype(jnp.float32)
        score = score - slope[None, :, :, None] * distance[:, None, None, None]
        return (update(carry, score, vb), None)

    state, _ = lax.scan(scan_step, state, (kblocks, vblocks, key_frames))
    kpos = key_start + jnp.arange(new_keys.shape[0], dtype=jnp.int32)
    kframe = (cache_frames + kpos // FRAME).astype(jnp.float32)
    score = (
        jnp.einsum("rgqd,kgd->rgqk", query, new_keys, preferred_element_type=jnp.float32) * scale
    )
    score = score - slope[None, :, :, None] * (qframe[:, None] - kframe[None, :])[:, None, None, :]
    visible = kpos[None, :] <= qpos[:, None]
    score = jnp.where(visible[:, None, None, :], score, -1e30)
    return update(state, score, new_values)


def combine_sources(acc, high, total):
    top = jnp.max(high, axis=0)
    scaling = jnp.exp(high - top[None])
    return jnp.sum(acc * scaling[..., None], axis=0) / jnp.sum(total * scaling, axis=0)[..., None]


def in_steps(queries, cache_keys, cache_values, new_keys, new_values, frame_of_slot, slopes):
    rows, local_heads, width = queries.shape
    groups = cache_keys.shape[1]
    group = local_heads // groups
    shards = lax.axis_size("ctx")
    position = lax.axis_index("ctx")
    cache_frames = frame_of_slot.shape[0] * shards
    parity = position % 2
    other = 1 - parity
    keep_keys = lax.dynamic_slice_in_dim(cache_keys, parity, 1, 1)
    keep_values = lax.dynamic_slice_in_dim(cache_values, parity, 1, 1)
    keep_new_keys = lax.dynamic_slice_in_dim(new_keys, parity, 1, 1)
    keep_new_values = lax.dynamic_slice_in_dim(new_values, parity, 1, 1)
    sent = (
        lax.dynamic_slice_in_dim(cache_keys, other, 1, 1),
        lax.dynamic_slice_in_dim(cache_values, other, 1, 1),
        lax.dynamic_slice_in_dim(new_keys, other, 1, 1),
        lax.dynamic_slice_in_dim(new_values, other, 1, 1),
    )
    got_keys, got_values, got_new_keys, got_new_values = from_partner(
        (sent[0], sent[1], sent[2], sent[3]), "ctx", 0
    )
    got_frames = from_partner(frame_of_slot, "ctx", 0)
    pair_keys = jnp.concatenate([keep_keys, got_keys], axis=0)
    pair_values = jnp.concatenate([keep_values, got_values], axis=0)
    pair_frames = jnp.concatenate([frame_of_slot, got_frames], axis=0)
    lower = parity == 0
    pair_new_keys = jnp.where(
        lower,
        jnp.concatenate([keep_new_keys, got_new_keys], axis=0),
        jnp.concatenate([got_new_keys, keep_new_keys], axis=0),
    )
    pair_new_values = jnp.where(
        lower,
        jnp.concatenate([keep_new_values, got_new_values], axis=0),
        jnp.concatenate([got_new_values, keep_new_values], axis=0),
    )
    pair_start = (position - parity) * new_keys.shape[0]
    split_heads = jnp.transpose(queries.reshape(rows, groups, group, width), (1, 0, 2, 3))
    outgoing = jnp.tile(split_heads, (shards // groups, 1, 1, 1))
    everyone = lax.all_to_all(outgoing, "ctx", split_axis=0, concat_axis=0, tiled=True).reshape(
        shards * rows, group, width
    )
    my_slopes = lax.dynamic_slice_in_dim(slopes, parity * group, group)
    count = rows * shards
    acc, high, total = attend(
        everyone,
        (
            jnp.zeros((count, 1, group, width), jnp.float32),
            jnp.full((count, 1, group), -1e30, jnp.float32),
            jnp.zeros((count, 1, group), jnp.float32),
        ),
        pair_keys,
        pair_values,
        pair_frames,
        pair_new_keys,
        pair_new_values,
        my_slopes,
        pair_start,
        cache_frames,
    )
    acc, high, total = (
        lax.all_to_all(acc, "ctx", split_axis=0, concat_axis=0, tiled=True),
        lax.all_to_all(high, "ctx", split_axis=0, concat_axis=0, tiled=True),
        lax.all_to_all(total, "ctx", split_axis=0, concat_axis=0, tiled=True),
    )
    acc = acc.reshape(shards // groups, groups, rows, group, width)
    high = high.reshape(shards // groups, groups, rows, group)
    total = total.reshape(shards // groups, groups, rows, group)
    merged = jnp.transpose(combine_sources(acc, high, total), (1, 0, 2, 3))
    result = merged.astype(jnp.bfloat16).reshape(rows, local_heads * width)
    return lax.all_gather(result, "head", axis=1, tiled=True)


def on_device(*arrays):
    fresh, local, width = arrays[0].shape
    cached = arrays[1].shape[0]
    frames = arrays[5].shape[0]
    shards, heads = lax.axis_size("ctx"), lax.axis_size("head")
    whole_tiles = fresh % 16 == 0 and cached % 16 == 0 and width % 128 == 0
    pairs = shards % 2 == 0 and shards > 2 and heads % 2 == 0
    if whole_tiles and pairs and frames == 1 and (local // arrays[1].shape[1]) % PARTS == 0:
        return in_one_kernel(*arrays)
    return in_steps(*arrays)


def solution(mesh):
    return jax.shard_map(
        on_device,
        mesh=mesh,
        in_specs=(
            P("ctx", "head", None),
            P("ctx", "head", None),
            P("ctx", "head", None),
            P("ctx", "head", None),
            P("ctx", "head", None),
            P("ctx"),
            P("head"),
        ),
        out_specs=P("ctx", None),
        check_vma=False,
    )
```

```python
import functools
import math

import jax
import jax.numpy as jnp
from jax import lax
from jax.experimental import pallas as pl
from jax.experimental.pallas import tpu as pltpu
from jax.sharding import PartitionSpec as P

FRAME = 256
FRAME_BITS = FRAME.bit_length() - 1
MESH = pl.DeviceIdType.MESH
LOG2E = 1.0 / math.log(2.0)
PARTS = 2


def nt(a, b):
    return lax.dot_general(a, b, (((1,), (1,)), ((), ())), preferred_element_type=jnp.float32)


def tn(a, b):
    return lax.dot_general(a, b, (((0,), (0,)), ((), ())), preferred_element_type=jnp.float32)


def iota(shape, dim):
    return lax.broadcasted_iota(jnp.int32, shape, dim)


def kernel(
    sizes,
    q_in,
    ck_in,
    cv_in,
    nk_in,
    nv_in,
    frame_in,
    slope_in,
    o_ref,
    q_ref,
    ck_ref,
    cv_ref,
    nk_ref,
    nv_ref,
    frame_ref,
    slope_ref,
    kv,
    qb,
    slope_rows,
    acc,
    high,
    total,
    part_out,
    part_in,
    in_sem,
    kv_up,
    kv_down,
    kv_recv,
    q_send,
    q_recv,
    p_send,
    p_recv,
    o_send,
    o_recv,
):
    cached, fresh, groups, group, width, shards, heads = sizes
    column = shards // 2
    rows = group * fresh
    cache_frames = shards
    position = lax.axis_index("ctx")
    me = lax.axis_index("head")
    side = position % 2
    place = position // 2
    across = position + 1 - 2 * side
    sibling = me + 1 - 2 * (me % 2)
    peers = [lax.rem(me + 2 * k, heads) for k in range(1, heads // 2)]
    last = column - 1
    has_up = place < last
    has_down = place > 0
    scale = LOG2E / width**0.5
    v_at = cached + fresh
    f_at = 2 * v_at

    fetches = [
        pltpu.make_async_copy(src, dst, in_sem.at[k])
        for k, (src, dst) in enumerate(
            (
                (ck_in, ck_ref),
                (nk_in, nk_ref),
                (cv_in, cv_ref),
                (nv_in, nv_ref),
                (frame_in, frame_ref),
                (q_in, q_ref),
                (slope_in, slope_ref),
            )
        )
    ]
    for fetch in fetches:
        fetch.start()

    barrier = pltpu.get_barrier_semaphore()
    pl.semaphore_signal(barrier, inc=1, device_id={"ctx": across}, device_id_type=MESH)
    for other in [sibling] + peers:
        pl.semaphore_signal(barrier, inc=1, device_id={"head": other}, device_id_type=MESH)

    @pl.when(has_up)
    def _():
        pl.semaphore_signal(barrier, inc=1, device_id={"ctx": position + 2}, device_id_type=MESH)

    @pl.when(has_down)
    def _():
        pl.semaphore_signal(barrier, inc=1, device_id={"ctx": position - 2}, device_id_type=MESH)

    for fetch in fetches[:5]:
        fetch.wait()
    frame = frame_ref[0].astype(jnp.float32)
    for g in range(groups):
        pick = (iota((cached, groups * cached), 1) == groups * iota((cached, groups * cached), 0) + g)
        pick = pick.astype(jnp.float32).astype(jnp.bfloat16)
        few = pick[:fresh, : groups * fresh]
        for src, at, sel, n in (
            (ck_ref, 0, pick, cached),
            (nk_ref, cached, few, fresh),
            (cv_ref, v_at, pick, cached),
            (nv_ref, v_at + cached, few, fresh),
        ):
            kv[place, g, at : at + n, :] = jnp.dot(
                sel, src[...], preferred_element_type=jnp.float32
            ).astype(jnp.bfloat16)
        kv[place, g, f_at : f_at + 16, :] = jnp.full((16, width), frame, jnp.float32).astype(
            jnp.bfloat16
        )

    pl.semaphore_wait(
        barrier, 1 + heads // 2 + jnp.minimum(place, 1) + jnp.minimum(last - place, 1)
    )

    def up(src, g):
        return pltpu.make_async_remote_copy(
            src_ref=kv.at[src, g],
            dst_ref=kv.at[src, g],
            send_sem=kv_up.at[src, g],
            recv_sem=kv_recv.at[src, g],
            device_id={"ctx": position + 2},
            device_id_type=MESH,
        )

    def down(src, g):
        return pltpu.make_async_remote_copy(
            src_ref=kv.at[src, g],
            dst_ref=kv.at[src, g],
            send_sem=kv_down.at[src, g],
            recv_sem=kv_recv.at[src, g],
            device_id={"ctx": position - 2},
            device_id_type=MESH,
        )

    for g in range(groups):

        @pl.when(has_up)
        def _():
            up(place, g).start()

        @pl.when(has_down)
        def _():
            down(place, g).start()

    def q_copy(g):
        return pltpu.make_async_remote_copy(
            src_ref=qb.at[0, g],
            dst_ref=qb.at[1, g],
            send_sem=q_send.at[g],
            recv_sem=q_recv.at[g],
            device_id={"ctx": across},
            device_id_type=MESH,
        )

    for fetch in fetches[5:]:
        fetch.wait()
    local = groups * group
    slant = iota((fresh, local * fresh), 1) - local * iota((fresh, local * fresh), 0)
    for g in range(groups):
        pick = jnp.concatenate(
            [
                (slant == g * group + j).astype(jnp.float32).astype(jnp.bfloat16)
                for j in range(group)
            ],
            axis=0,
        )
        qb[0, g] = jnp.dot(pick, q_ref[...], preferred_element_type=jnp.float32).astype(jnp.bfloat16)
        q_copy(g).start()

    token = iota((1, rows), 1)
    for g in range(groups):
        row = jnp.full((1, rows), slope_ref[g * group])
        for j in range(1, group):
            row = jnp.where(token >= j * fresh, slope_ref[g * group + j], row)
        slope_rows[g] = row * LOG2E
    for j in range(group - 1, 0, -1):
        token = jnp.where(token >= j * fresh, token - j * fresh, token)

    def query_position(r):
        owner = position if r == 0 else across
        return owner * fresh + token

    def frame_of(positions):
        return (cache_frames + jnp.right_shift(positions, FRAME_BITS)).astype(jnp.float32)

    for i in range(2 * groups):
        acc[i] = jnp.zeros((width, rows), jnp.float32)
        high[i] = jnp.full((1, rows), -1e30, jnp.float32)
        total[i] = jnp.zeros((1, rows), jnp.float32)

    def attend(src, g, sides=(1, 0)):
        keys = kv[src, g, 0:v_at, :]
        values = kv[src, g, v_at:f_at, :]
        key_frame = kv[src, g, f_at : f_at + 16, :].astype(jnp.float32)[0:1, 0:1]
        key_position = iota((fresh, 1), 0) + (2 * src + side) * fresh
        new_frame = frame_of(key_position)
        slope = slope_rows[g]
        before = [(high[2 * g + r], total[2 * g + r], acc[2 * g + r]) for r in sides]
        after = []
        for r, (top, sums, out) in zip(sides, before):
            score = nt(keys, qb[r, g]) * scale
            here = query_position(r)
            shift = slope * (key_frame - frame_of(here))
            old = score[:cached]
            new = score[cached:] + slope * (new_frame - frame_of(here))
            new = jnp.where(key_position <= here, new, -1e30)
            now = jnp.maximum(
                jnp.max(old, axis=0, keepdims=True) + shift, jnp.max(new, axis=0, keepdims=True)
            )
            now = jnp.maximum(top, now)
            corr = jnp.exp2(top - now)
            old = jnp.exp2(old + (shift - now))
            new = jnp.exp2(new - now)
            sums = sums * corr + (
                jnp.sum(old, axis=0, keepdims=True) + jnp.sum(new, axis=0, keepdims=True)
            )
            weight = jnp.concatenate([old.astype(jnp.bfloat16), new.astype(jnp.bfloat16)], axis=0)
            after.append((now, sums, out * corr + tn(values, weight)))
        for r, (now, sums, out) in zip(sides, after):
            high[2 * g + r] = now
            total[2 * g + r] = sums
            acc[2 * g + r] = out

    def pass_on(apart, g):
        low = place - apart
        top = place + apart

        @pl.when(low >= 0)
        def _():
            up(low, g).wait_recv()

            @pl.when(has_up)
            def _():
                up(low, g).start()

        @pl.when(top <= last)
        def _():
            down(top, g).wait_recv()

            @pl.when(has_down)
            def _():
                down(top, g).start()

    def attend_pair(apart, g, sides=(1, 0)):
        low = place - apart
        top = place + apart

        @pl.when(low >= 0)
        def _():
            attend(low, g, sides)

        @pl.when(top <= last)
        def _():
            attend(top, g, sides)

    part_rows = rows // PARTS
    part_heads = group // PARTS

    def p_copy(i):
        return pltpu.make_async_remote_copy(
            src_ref=part_out.at[i],
            dst_ref=part_in.at[i],
            send_sem=p_send.at[i],
            recv_sem=p_recv.at[i],
            device_id={"ctx": across},
            device_id_type=MESH,
        )

    def finish(g):
        sub = iota((16, part_rows), 0)
        for c in range(PARTS):
            i = g * PARTS + c
            cols = slice(c * part_rows, (c + 1) * part_rows)
            sums = total[2 * g + 1, :, cols]
            part_out[i, 0:width, :] = (acc[2 * g + 1, :, cols] * (1.0 / sums)).astype(jnp.bfloat16)
            lse = high[2 * g + 1, :, cols] + jnp.log(sums) * LOG2E
            one = lse.astype(jnp.bfloat16).astype(jnp.float32)
            two = (lse - one).astype(jnp.bfloat16).astype(jnp.float32)
            three = lse - one - two
            stats = jnp.where(sub == 0, one, jnp.where(sub == 1, two, three))
            part_out[i, width : width + 16, :] = stats.astype(jnp.bfloat16)
            p_copy(i).start()

    def block_of(owner, i):
        at = (owner * groups * PARTS + i) * part_heads * width
        return o_ref.at[:, pl.ds(pl.multiple_of(at, part_heads * width), part_heads * width)]

    def o_copy(owner, i, slot, target):
        return pltpu.make_async_remote_copy(
            src_ref=block_of(owner, i),
            dst_ref=block_of(owner, i),
            send_sem=o_send.at[slot, i],
            recv_sem=o_recv.at[owner, i],
            device_id={"head": target},
            device_id_type=MESH,
        )

    def combine(i):
        g, c = divmod(i, PARTS)
        cols = slice(c * part_rows, (c + 1) * part_rows)
        sums = total[2 * g, :, cols]
        mine = high[2 * g, :, cols] + jnp.log(sums) * LOG2E
        p_copy(i).wait_recv()
        stats = part_in[i, width : width + 16, :].astype(jnp.float32)
        theirs = stats[0:1] + stats[1:2] + stats[2:3]
        top = jnp.maximum(mine, theirs)
        a = jnp.exp2(mine - top)
        b = jnp.exp2(theirs - top)
        both = a + b
        out = acc[2 * g, :, cols] * (a / (sums * both)) + part_in[i, 0:width, :].astype(
            jnp.float32
        ) * (b / both)
        out = out.T
        at = (me * groups * PARTS + i) * part_heads * width
        for j in range(part_heads):
            spot = pl.multiple_of(at + j * width, width)
            o_ref[:, pl.ds(spot, width)] = out[j * fresh : (j + 1) * fresh].astype(jnp.bfloat16)
        for k, peer in enumerate(peers):
            o_copy(me, i, 1 + k, peer).start()
        o_copy(me, i, 0, sibling).start()

    def forward(i):
        for k, peer in enumerate(peers):
            o_copy(peer, i, 0, sibling).wait_recv()
            o_copy(peer, i, 1 + len(peers) + k, sibling).start()

    steps = groups * last

    def body(it, carry):
        apart = it // groups + 1
        g = it % groups
        pass_on(apart, g)

        @pl.when(apart == 1)
        def _():
            q_copy(g).wait_recv()
            attend(place, g)

        attend_pair(apart, g)
        return carry

    lax.fori_loop(0, steps - groups + 1, body, 0)
    finish(0)
    for g in range(1, groups):
        pass_on(last, g)
        attend_pair(last, g, (1,))
        finish(g)
        attend_pair(last, g, (0,))

    count = groups * PARTS
    behind = PARTS
    for i in range(count):
        combine(i)
        if i >= behind:
            forward(i - behind)
    for i in range(count - behind, count):
        forward(i)
    for i in range(count):
        o_copy(sibling, i, 0, sibling).wait_recv()
        for peer in peers:
            far = peer + 1 - 2 * (peer % 2)
            o_copy(far, i, 0, sibling).wait_recv()

    for g in range(groups):
        for src in range(column):

            @pl.when(jnp.logical_and(has_up, src <= place))
            def _():
                up(src, g).wait_send()

            @pl.when(jnp.logical_and(has_down, src >= place))
            def _():
                down(src, g).wait_send()

        q_copy(g).wait_send()
    for i in range(count):
        p_copy(i).wait_send()
        o_copy(me, i, 0, sibling).wait_send()
        for k, peer in enumerate(peers):
            o_copy(me, i, 1 + k, peer).wait_send()
            o_copy(peer, i, 1 + len(peers) + k, sibling).wait_send()


def in_one_kernel(queries, cache_keys, cache_values, new_keys, new_values, frame_of_slot, slopes):
    fresh, local, width = queries.shape
    cached, groups, _ = cache_keys.shape
    group = local // groups
    shards = lax.axis_size("ctx")
    heads = lax.axis_size("head")
    column = shards // 2
    rows = group * fresh
    slab = 2 * (cached + fresh) + 16
    count = groups * PARTS
    vmem = pl.BlockSpec(memory_space=pltpu.VMEM)
    dma = pltpu.SemaphoreType.DMA
    sizes = (cached, fresh, groups, group, width, shards, heads)
    return pl.pallas_call(
        functools.partial(kernel, sizes),
        out_shape=jax.ShapeDtypeStruct((fresh, heads * local * width), jnp.bfloat16),
        in_specs=[pl.BlockSpec(memory_space=pl.ANY)] * 7,
        out_specs=vmem,
        scratch_shapes=[
            pltpu.VMEM((fresh * local, width), jnp.bfloat16),
            pltpu.VMEM((cached * groups, width), jnp.bfloat16),
            pltpu.VMEM((cached * groups, width), jnp.bfloat16),
            pltpu.VMEM((fresh * groups, width), jnp.bfloat16),
            pltpu.VMEM((fresh * groups, width), jnp.bfloat16),
            pltpu.SMEM(frame_of_slot.shape, jnp.int32),
            pltpu.SMEM(slopes.shape, jnp.float32),
            pltpu.VMEM((column, groups, slab, width), jnp.bfloat16),
            pltpu.VMEM((2, groups, rows, width), jnp.bfloat16),
            pltpu.VMEM((groups, 1, rows), jnp.float32),
            pltpu.VMEM((2 * groups, width, rows), jnp.float32),
            pltpu.VMEM((2 * groups, 1, rows), jnp.float32),
            pltpu.VMEM((2 * groups, 1, rows), jnp.float32),
            pltpu.VMEM((count, width + 16, rows // PARTS), jnp.bfloat16),
            pltpu.VMEM((count, width + 16, rows // PARTS), jnp.bfloat16),
            dma((7,)),
            dma((column, groups)),
            dma((column, groups)),
            dma((column, groups)),
            dma((groups,)),
            dma((groups,)),
            dma((count,)),
            dma((count,)),
            dma((heads - 1, count)),
            dma((heads, count)),
        ],
        compiler_params=pltpu.CompilerParams(
            collective_id=0, has_side_effects=True, vmem_limit_bytes=64 * 1024 * 1024
        ),
        name="attend_over_slice",
    )(
        queries.reshape(fresh * local, width),
        cache_keys.reshape(cached * groups, width),
        cache_values.reshape(cached * groups, width),
        new_keys.reshape(fresh * groups, width),
        new_values.reshape(fresh * groups, width),
        frame_of_slot,
        slopes,
    )


def from_partner(value, axis, apart):
    return lax.ppermute(value, axis, [(i, i ^ 1 << apart) for i in range(lax.axis_size(axis))])


def update(state, score, values):
    acc, high, total = state
    new_high = jnp.maximum(high, jnp.max(score, axis=-1))
    corr = jnp.exp(high - new_high)
    expo = jnp.exp(score - new_high[..., None])
    total = total * corr + jnp.sum(expo, axis=-1)
    weight = expo.astype(jnp.bfloat16)
    acc = acc * corr[..., None] + jnp.einsum(
        "rgqk,kgd->rgqd", weight, values, preferred_element_type=jnp.float32
    )
    return (acc, new_high, total)


def attend(
    q_rows,
    state,
    cache_keys,
    cache_values,
    key_frames,
    new_keys,
    new_values,
    slopes,
    key_start,
    cache_frames,
):
    rows, local_heads, width = q_rows.shape
    groups = cache_keys.shape[1]
    group = local_heads // groups
    scale = 1.0 / width**0.5
    query = q_rows.reshape(rows, groups, group, width)
    qpos = jnp.arange(rows, dtype=jnp.int32)
    qframe = (cache_frames + qpos // FRAME).astype(jnp.float32)
    slope = slopes.reshape(groups, group)
    frames = key_frames.shape[0]
    kblocks = cache_keys.reshape(frames, FRAME, groups, width)
    vblocks = cache_values.reshape(frames, FRAME, groups, width)

    def scan_step(carry, items):
        kb, vb, fb = items
        score = jnp.einsum("rgqd,kgd->rgqk", query, kb, preferred_element_type=jnp.float32) * scale
        distance = qframe - fb.astype(jnp.float32)
        score = score - slope[None, :, :, None] * distance[:, None, None, None]
        return (update(carry, score, vb), None)

    state, _ = lax.scan(scan_step, state, (kblocks, vblocks, key_frames))
    kpos = key_start + jnp.arange(new_keys.shape[0], dtype=jnp.int32)
    kframe = (cache_frames + kpos // FRAME).astype(jnp.float32)
    score = (
        jnp.einsum("rgqd,kgd->rgqk", query, new_keys, preferred_element_type=jnp.float32) * scale
    )
    score = score - slope[None, :, :, None] * (qframe[:, None] - kframe[None, :])[:, None, None, :]
    visible = kpos[None, :] <= qpos[:, None]
    score = jnp.where(visible[:, None, None, :], score, -1e30)
    return update(state, score, new_values)


def combine_sources(acc, high, total):
    top = jnp.max(high, axis=0)
    scaling = jnp.exp(high - top[None])
    return jnp.sum(acc * scaling[..., None], axis=0) / jnp.sum(total * scaling, axis=0)[..., None]


def in_steps(queries, cache_keys, cache_values, new_keys, new_values, frame_of_slot, slopes):
    rows, local_heads, width = queries.shape
    groups = cache_keys.shape[1]
    group = local_heads // groups
    shards = lax.axis_size("ctx")
    position = lax.axis_index("ctx")
    cache_frames = frame_of_slot.shape[0] * shards
    parity = position % 2
    other = 1 - parity
    keep_keys = lax.dynamic_slice_in_dim(cache_keys, parity, 1, 1)
    keep_values = lax.dynamic_slice_in_dim(cache_values, parity, 1, 1)
    keep_new_keys = lax.dynamic_slice_in_dim(new_keys, parity, 1, 1)
    keep_new_values = lax.dynamic_slice_in_dim(new_values, parity, 1, 1)
    sent = (
        lax.dynamic_slice_in_dim(cache_keys, other, 1, 1),
        lax.dynamic_slice_in_dim(cache_values, other, 1, 1),
        lax.dynamic_slice_in_dim(new_keys, other, 1, 1),
        lax.dynamic_slice_in_dim(new_values, other, 1, 1),
    )
    got_keys, got_values, got_new_keys, got_new_values = from_partner(
        (sent[0], sent[1], sent[2], sent[3]), "ctx", 0
    )
    got_frames = from_partner(frame_of_slot, "ctx", 0)
    pair_keys = jnp.concatenate([keep_keys, got_keys], axis=0)
    pair_values = jnp.concatenate([keep_values, got_values], axis=0)
    pair_frames = jnp.concatenate([frame_of_slot, got_frames], axis=0)
    lower = parity == 0
    pair_new_keys = jnp.where(
        lower,
        jnp.concatenate([keep_new_keys, got_new_keys], axis=0),
        jnp.concatenate([got_new_keys, keep_new_keys], axis=0),
    )
    pair_new_values = jnp.where(
        lower,
        jnp.concatenate([keep_new_values, got_new_values], axis=0),
        jnp.concatenate([got_new_values, keep_new_values], axis=0),
    )
    pair_start = (position - parity) * new_keys.shape[0]
    split_heads = jnp.transpose(queries.reshape(rows, groups, group, width), (1, 0, 2, 3))
    outgoing = jnp.tile(split_heads, (shards // groups, 1, 1, 1))
    everyone = lax.all_to_all(outgoing, "ctx", split_axis=0, concat_axis=0, tiled=True).reshape(
        shards * rows, group, width
    )
    my_slopes = lax.dynamic_slice_in_dim(slopes, parity * group, group)
    count = rows * shards
    acc, high, total = attend(
        everyone,
        (
            jnp.zeros((count, 1, group, width), jnp.float32),
            jnp.full((count, 1, group), -1e30, jnp.float32),
            jnp.zeros((count, 1, group), jnp.float32),
        ),
        pair_keys,
        pair_values,
        pair_frames,
        pair_new_keys,
        pair_new_values,
        my_slopes,
        pair_start,
        cache_frames,
    )
    acc, high, total = (
        lax.all_to_all(acc, "ctx", split_axis=0, concat_axis=0, tiled=True),
        lax.all_to_all(high, "ctx", split_axis=0, concat_axis=0, tiled=True),
        lax.all_to_all(total, "ctx", split_axis=0, concat_axis=0, tiled=True),
    )
    acc = acc.reshape(shards // groups, groups, rows, group, width)
    high = high.reshape(shards // groups, groups, rows, group)
    total = total.reshape(shards // groups, groups, rows, group)
    merged = jnp.transpose(combine_sources(acc, high, total), (1, 0, 2, 3))
    result = merged.astype(jnp.bfloat16).reshape(rows, local_heads * width)
    return lax.all_gather(result, "head", axis=1, tiled=True)


def on_device(*arrays):
    fresh, local, width = arrays[0].shape
    cached = arrays[1].shape[0]
    frames = arrays[5].shape[0]
    shards, heads = lax.axis_size("ctx"), lax.axis_size("head")
    whole_tiles = fresh % 16 == 0 and cached % 16 == 0 and width % 128 == 0
    pairs = shards % 2 == 0 and shards > 2 and heads % 2 == 0
    if whole_tiles and pairs and frames == 1 and (local // arrays[1].shape[1]) % PARTS == 0:
        return in_one_kernel(*arrays)
    return in_steps(*arrays)


def solution(mesh):
    return jax.shard_map(
        on_device,
        mesh=mesh,
        in_specs=(
            P("ctx", "head", None),
            P("ctx", "head", None),
            P("ctx", "head", None),
            P("ctx", "head", None),
            P("ctx", "head", None),
            P("ctx"),
            P("head"),
        ),
        out_specs=P("ctx", None),
        check_vma=False,
    )
```

```python
import functools
import math

import jax
import jax.numpy as jnp
from jax import lax
from jax.experimental import pallas as pl
from jax.experimental.pallas import tpu as pltpu
from jax.sharding import PartitionSpec as P

FRAME = 256
FRAME_BITS = FRAME.bit_length() - 1
MESH = pl.DeviceIdType.MESH
LOG2E = 1.0 / math.log(2.0)
PARTS = 4


def nt(a, b):
    return lax.dot_general(a, b, (((1,), (1,)), ((), ())), preferred_element_type=jnp.float32)


def iota(shape, dim):
    return lax.broadcasted_iota(jnp.int32, shape, dim)


def kernel(
    sizes,
    q_in,
    ck_in,
    cv_in,
    nk_in,
    nv_in,
    frame_in,
    slope_in,
    o_ref,
    q_ref,
    ck_ref,
    cv_ref,
    nk_ref,
    nv_ref,
    frame_ref,
    slope_ref,
    kv,
    qb,
    slope_rows,
    acc,
    high,
    total,
    part_out,
    part_in,
    in_sem,
    kv_up,
    kv_down,
    kv_recv,
    q_send,
    q_recv,
    p_send,
    p_recv,
    o_send,
    o_recv,
):
    cached, fresh, groups, group, width, shards, heads = sizes
    column = shards // 2
    rows = group * fresh
    cache_frames = shards
    position = lax.axis_index("ctx")
    me = lax.axis_index("head")
    side = position % 2
    place = position // 2
    across = position + 1 - 2 * side
    sibling = me + 1 - 2 * (me % 2)
    peers = [lax.rem(me + 2 * k, heads) for k in range(1, heads // 2)]
    last = column - 1
    has_up = place < last
    has_down = place > 0
    scale = LOG2E / width**0.5
    k_at = fresh
    f_at = fresh + cached
    v_at = f_at + 16
    n_at = v_at + cached
    old_rows = slice(k_at, n_at)

    fetches = [
        pltpu.make_async_copy(src, dst, in_sem.at[k])
        for k, (src, dst) in enumerate(
            (
                (ck_in, ck_ref),
                (nk_in, nk_ref),
                (cv_in, cv_ref),
                (nv_in, nv_ref),
                (frame_in, frame_ref),
                (q_in, q_ref),
                (slope_in, slope_ref),
            )
        )
    ]
    for fetch in fetches:
        fetch.start()

    barrier = pltpu.get_barrier_semaphore()
    pl.semaphore_signal(barrier, inc=1, device_id={"ctx": across}, device_id_type=MESH)
    for other in [sibling] + peers:
        pl.semaphore_signal(barrier, inc=1, device_id={"head": other}, device_id_type=MESH)

    @pl.when(has_up)
    def _():
        pl.semaphore_signal(barrier, inc=1, device_id={"ctx": position + 2}, device_id_type=MESH)

    @pl.when(has_down)
    def _():
        pl.semaphore_signal(barrier, inc=1, device_id={"ctx": position - 2}, device_id_type=MESH)

    def up(src, g):
        return pltpu.make_async_remote_copy(
            src_ref=kv.at[src, g],
            dst_ref=kv.at[src, g],
            send_sem=kv_up.at[src, g],
            recv_sem=kv_recv.at[src, g],
            device_id={"ctx": position + 2},
            device_id_type=MESH,
        )

    def down(src, g):
        return pltpu.make_async_remote_copy(
            src_ref=kv.at[src, g, old_rows],
            dst_ref=kv.at[src, g, old_rows],
            send_sem=kv_down.at[src, g],
            recv_sem=kv_recv.at[src, g],
            device_id={"ctx": position - 2},
            device_id_type=MESH,
        )

    for fetch in fetches[:5]:
        fetch.wait()
    frame = frame_ref[0].astype(jnp.float32)
    slant = iota((cached, groups * cached), 1) - groups * iota((cached, groups * cached), 0)
    for g in range(groups):
        pick = (slant == g).astype(jnp.float32).astype(jnp.bfloat16)
        few = pick[:fresh, : groups * fresh]
        for src, at, sel, n in (
            (nk_ref, 0, few, fresh),
            (ck_ref, k_at, pick, cached),
            (cv_ref, v_at, pick, cached),
            (nv_ref, n_at, few, fresh),
        ):
            kv[place, g, at : at + n, :] = jnp.dot(
                sel, src[...], preferred_element_type=jnp.float32
            ).astype(jnp.bfloat16)
        kv[place, g, f_at:v_at, :] = jnp.full((16, width), frame, jnp.float32).astype(jnp.bfloat16)
        if g == 0:
            pl.semaphore_wait(
                barrier, 1 + heads // 2 + jnp.minimum(place, 1) + jnp.minimum(last - place, 1)
            )

        @pl.when(has_up)
        def _():
            up(place, g).start()

        @pl.when(has_down)
        def _():
            down(place, g).start()

    def q_copy(g):
        return pltpu.make_async_remote_copy(
            src_ref=qb.at[0, g],
            dst_ref=qb.at[1, g],
            send_sem=q_send.at[g],
            recv_sem=q_recv.at[g],
            device_id={"ctx": across},
            device_id_type=MESH,
        )

    for fetch in fetches[5:]:
        fetch.wait()
    local = groups * group
    slant = iota((fresh, local * fresh), 1) - local * iota((fresh, local * fresh), 0)
    for g in range(groups):
        pick = jnp.concatenate(
            [
                (slant == g * group + j).astype(jnp.float32).astype(jnp.bfloat16)
                for j in range(group)
            ],
            axis=0,
        )
        qb[0, g] = jnp.dot(pick, q_ref[...], preferred_element_type=jnp.float32).astype(jnp.bfloat16)
        q_copy(g).start()

    token = iota((1, rows), 1)
    for g in range(groups):
        row = jnp.full((1, rows), slope_ref[g * group])
        for j in range(1, group):
            row = jnp.where(token >= j * fresh, slope_ref[g * group + j], row)
        slope_rows[g] = row * LOG2E
    for j in range(group - 1, 0, -1):
        token = jnp.where(token >= j * fresh, token - j * fresh, token)

    def query_position(r):
        owner = position if r == 0 else across
        return owner * fresh + token

    def frame_of(positions):
        return (cache_frames + jnp.right_shift(positions, FRAME_BITS)).astype(jnp.float32)

    for i in range(2 * groups):
        acc[i] = jnp.zeros((width, rows), jnp.float32)
        high[i] = jnp.full((1, rows), -1e30, jnp.float32)
        total[i] = jnp.zeros((1, rows), jnp.float32)

    def attend(src, g, sides, seen):
        keys = kv[src, g, 0 if seen else k_at : f_at, :]
        values = kv[src, g, v_at : n_at + fresh if seen else n_at, :].T
        key_frame = kv[src, g, f_at:v_at, :].astype(jnp.float32)[0:1, 0:1]
        key_position = iota((fresh, 1), 0) + (2 * src + side) * fresh
        new_frame = frame_of(key_position)
        slope = slope_rows[g]
        before = [(high[2 * g + r], total[2 * g + r], acc[2 * g + r]) for r in sides]
        after = []
        for r, (top, sums, out) in zip(sides, before):
            score = nt(keys, qb[r, g]) * scale
            here = query_position(r)
            shift = slope * (key_frame - frame_of(here))
            old = score[fresh:] if seen else score
            now = jnp.maximum(top, jnp.max(old, axis=0, keepdims=True) + shift)
            if seen:
                new = score[:fresh] + slope * (new_frame - frame_of(here))
                new = jnp.where(key_position <= here, new, -1e30)
                now = jnp.maximum(now, jnp.max(new, axis=0, keepdims=True))
            corr = jnp.exp2(top - now)
            old = jnp.exp2(old + (shift - now))
            fresh_sum = jnp.sum(old, axis=0, keepdims=True)
            weight = old.astype(jnp.bfloat16)
            if seen:
                new = jnp.exp2(new - now)
                fresh_sum = fresh_sum + jnp.sum(new, axis=0, keepdims=True)
                weight = jnp.concatenate([weight, new.astype(jnp.bfloat16)], axis=0)
            out = out * corr + jnp.dot(values, weight, preferred_element_type=jnp.float32)
            after.append((now, sums * corr + fresh_sum, out))
        for r, (now, sums, out) in zip(sides, after):
            high[2 * g + r] = now
            total[2 * g + r] = sums
            acc[2 * g + r] = out

    def pass_on(apart, g):
        low = place - apart
        top = place + apart

        @pl.when(low >= 0)
        def _():
            up(low, g).wait_recv()

            @pl.when(has_up)
            def _():
                up(low, g).start()

        @pl.when(top <= last)
        def _():
            down(top, g).wait_recv()

            @pl.when(has_down)
            def _():
                down(top, g).start()

    def attend_pair(apart, g, sides=(1, 0)):
        low = place - apart
        top = place + apart

        @pl.when(low >= 0)
        def _():
            attend(low, g, sides, True)

        @pl.when(top <= last)
        def _():
            attend(top, g, sides, False)

    part_rows = rows // PARTS
    part_heads = group // PARTS

    def p_copy(i):
        return pltpu.make_async_remote_copy(
            src_ref=part_out.at[i],
            dst_ref=part_in.at[i],
            send_sem=p_send.at[i],
            recv_sem=p_recv.at[i],
            device_id={"ctx": across},
            device_id_type=MESH,
        )

    def finish(g):
        sub = iota((16, part_rows), 0)
        for c in range(PARTS):
            i = g * PARTS + c
            cols = slice(c * part_rows, (c + 1) * part_rows)
            sums = total[2 * g + 1, :, cols]
            part_out[i, 0:width, :] = (acc[2 * g + 1, :, cols] * (1.0 / sums)).astype(jnp.bfloat16)
            lse = high[2 * g + 1, :, cols] + jnp.log(sums) * LOG2E
            one = lse.astype(jnp.bfloat16).astype(jnp.float32)
            two = (lse - one).astype(jnp.bfloat16).astype(jnp.float32)
            three = lse - one - two
            stats = jnp.where(sub == 0, one, jnp.where(sub == 1, two, three))
            part_out[i, width : width + 16, :] = stats.astype(jnp.bfloat16)
            p_copy(i).start()

    def block_of(owner, i):
        at = (owner * groups * PARTS + i) * part_heads * width
        return o_ref.at[:, pl.ds(pl.multiple_of(at, part_heads * width), part_heads * width)]

    def o_copy(owner, i, slot, target):
        return pltpu.make_async_remote_copy(
            src_ref=block_of(owner, i),
            dst_ref=block_of(owner, i),
            send_sem=o_send.at[slot, i],
            recv_sem=o_recv.at[owner, i],
            device_id={"head": target},
            device_id_type=MESH,
        )

    def combine(i):
        g, c = divmod(i, PARTS)
        cols = slice(c * part_rows, (c + 1) * part_rows)
        sums = total[2 * g, :, cols]
        mine = high[2 * g, :, cols] + jnp.log(sums) * LOG2E
        p_copy(i).wait_recv()
        stats = part_in[i, width : width + 16, :].astype(jnp.float32)
        theirs = stats[0:1] + stats[1:2] + stats[2:3]
        top = jnp.maximum(mine, theirs)
        a = jnp.exp2(mine - top)
        b = jnp.exp2(theirs - top)
        both = a + b
        out = acc[2 * g, :, cols] * (a / (sums * both)) + part_in[i, 0:width, :].astype(
            jnp.float32
        ) * (b / both)
        out = out.T
        at = (me * groups * PARTS + i) * part_heads * width
        for j in range(part_heads):
            spot = pl.multiple_of(at + j * width, width)
            o_ref[:, pl.ds(spot, width)] = out[j * fresh : (j + 1) * fresh].astype(jnp.bfloat16)
        for k, peer in enumerate(peers):
            o_copy(me, i, 1 + k, peer).start()
        o_copy(me, i, 0, sibling).start()

    def forward(i):
        for k, peer in enumerate(peers):
            o_copy(peer, i, 0, sibling).wait_recv()
            o_copy(peer, i, 1 + len(peers) + k, sibling).start()

    steps = groups * last

    def body(it, carry):
        apart = it // groups + 1
        g = it % groups
        pass_on(apart, g)

        @pl.when(apart == 1)
        def _():
            q_copy(g).wait_recv()
            attend(place, g, (1,), True)

        attend_pair(apart, g)
        return carry

    for g in range(groups):
        attend(place, g, (0,), True)
    lax.fori_loop(0, steps - groups, body, 0)
    for g in range(groups):
        pass_on(last, g)
        attend_pair(last, g, (1,))
        finish(g)
        if g > 0:
            for c in range(PARTS):
                combine((g - 1) * PARTS + c)
        attend_pair(last, g, (0,))

    count = groups * PARTS
    for c in range(PARTS):
        combine(count - PARTS + c)
        for g in range(groups - 1):
            forward(g * PARTS + c)
    for i in range(count - PARTS, count):
        forward(i)
    for i in range(count):
        o_copy(sibling, i, 0, sibling).wait_recv()
        for peer in peers:
            far = peer + 1 - 2 * (peer % 2)
            o_copy(far, i, 0, sibling).wait_recv()

    for g in range(groups):
        for src in range(column):

            @pl.when(jnp.logical_and(has_up, src <= place))
            def _():
                up(src, g).wait_send()

            @pl.when(jnp.logical_and(has_down, src >= place))
            def _():
                down(src, g).wait_send()

        q_copy(g).wait_send()
    for i in range(count):
        p_copy(i).wait_send()
        o_copy(me, i, 0, sibling).wait_send()
        for k, peer in enumerate(peers):
            o_copy(me, i, 1 + k, peer).wait_send()
            o_copy(peer, i, 1 + len(peers) + k, sibling).wait_send()


def in_one_kernel(queries, cache_keys, cache_values, new_keys, new_values, frame_of_slot, slopes):
    fresh, local, width = queries.shape
    cached, groups, _ = cache_keys.shape
    group = local // groups
    shards = lax.axis_size("ctx")
    heads = lax.axis_size("head")
    column = shards // 2
    rows = group * fresh
    slab = 2 * (cached + fresh) + 16
    count = groups * PARTS
    vmem = pl.BlockSpec(memory_space=pltpu.VMEM)
    dma = pltpu.SemaphoreType.DMA
    sizes = (cached, fresh, groups, group, width, shards, heads)
    return pl.pallas_call(
        functools.partial(kernel, sizes),
        out_shape=jax.ShapeDtypeStruct((fresh, heads * local * width), jnp.bfloat16),
        in_specs=[pl.BlockSpec(memory_space=pl.ANY)] * 7,
        out_specs=vmem,
        scratch_shapes=[
            pltpu.VMEM((fresh * local, width), jnp.bfloat16),
            pltpu.VMEM((cached * groups, width), jnp.bfloat16),
            pltpu.VMEM((cached * groups, width), jnp.bfloat16),
            pltpu.VMEM((fresh * groups, width), jnp.bfloat16),
            pltpu.VMEM((fresh * groups, width), jnp.bfloat16),
            pltpu.SMEM(frame_of_slot.shape, jnp.int32),
            pltpu.SMEM(slopes.shape, jnp.float32),
            pltpu.VMEM((column, groups, slab, width), jnp.bfloat16),
            pltpu.VMEM((2, groups, rows, width), jnp.bfloat16),
            pltpu.VMEM((groups, 1, rows), jnp.float32),
            pltpu.VMEM((2 * groups, width, rows), jnp.float32),
            pltpu.VMEM((2 * groups, 1, rows), jnp.float32),
            pltpu.VMEM((2 * groups, 1, rows), jnp.float32),
            pltpu.VMEM((count, width + 16, rows // PARTS), jnp.bfloat16),
            pltpu.VMEM((count, width + 16, rows // PARTS), jnp.bfloat16),
            dma((7,)),
            dma((column, groups)),
            dma((column, groups)),
            dma((column, groups)),
            dma((groups,)),
            dma((groups,)),
            dma((count,)),
            dma((count,)),
            dma((heads - 1, count)),
            dma((heads, count)),
        ],
        compiler_params=pltpu.CompilerParams(
            collective_id=0, has_side_effects=True, vmem_limit_bytes=62 * 1024 * 1024
        ),
        name="attend_over_slice",
    )(
        queries.reshape(fresh * local, width),
        cache_keys.reshape(cached * groups, width),
        cache_values.reshape(cached * groups, width),
        new_keys.reshape(fresh * groups, width),
        new_values.reshape(fresh * groups, width),
        frame_of_slot,
        slopes,
    )


def from_partner(value, axis, apart):
    return lax.ppermute(value, axis, [(i, i ^ 1 << apart) for i in range(lax.axis_size(axis))])


def update(state, score, values):
    acc, high, total = state
    new_high = jnp.maximum(high, jnp.max(score, axis=-1))
    corr = jnp.exp(high - new_high)
    expo = jnp.exp(score - new_high[..., None])
    total = total * corr + jnp.sum(expo, axis=-1)
    weight = expo.astype(jnp.bfloat16)
    acc = acc * corr[..., None] + jnp.einsum(
        "rgqk,kgd->rgqd", weight, values, preferred_element_type=jnp.float32
    )
    return (acc, new_high, total)


def attend(
    q_rows,
    state,
    cache_keys,
    cache_values,
    key_frames,
    new_keys,
    new_values,
    slopes,
    key_start,
    cache_frames,
):
    rows, local_heads, width = q_rows.shape
    groups = cache_keys.shape[1]
    group = local_heads // groups
    scale = 1.0 / width**0.5
    query = q_rows.reshape(rows, groups, group, width)
    qpos = jnp.arange(rows, dtype=jnp.int32)
    qframe = (cache_frames + qpos // FRAME).astype(jnp.float32)
    slope = slopes.reshape(groups, group)
    frames = key_frames.shape[0]
    kblocks = cache_keys.reshape(frames, FRAME, groups, width)
    vblocks = cache_values.reshape(frames, FRAME, groups, width)

    def scan_step(carry, items):
        kb, vb, fb = items
        score = jnp.einsum("rgqd,kgd->rgqk", query, kb, preferred_element_type=jnp.float32) * scale
        distance = qframe - fb.astype(jnp.float32)
        score = score - slope[None, :, :, None] * distance[:, None, None, None]
        return (update(carry, score, vb), None)

    state, _ = lax.scan(scan_step, state, (kblocks, vblocks, key_frames))
    kpos = key_start + jnp.arange(new_keys.shape[0], dtype=jnp.int32)
    kframe = (cache_frames + kpos // FRAME).astype(jnp.float32)
    score = (
        jnp.einsum("rgqd,kgd->rgqk", query, new_keys, preferred_element_type=jnp.float32) * scale
    )
    score = score - slope[None, :, :, None] * (qframe[:, None] - kframe[None, :])[:, None, None, :]
    visible = kpos[None, :] <= qpos[:, None]
    score = jnp.where(visible[:, None, None, :], score, -1e30)
    return update(state, score, new_values)


def combine_sources(acc, high, total):
    top = jnp.max(high, axis=0)
    scaling = jnp.exp(high - top[None])
    return jnp.sum(acc * scaling[..., None], axis=0) / jnp.sum(total * scaling, axis=0)[..., None]


def in_steps(queries, cache_keys, cache_values, new_keys, new_values, frame_of_slot, slopes):
    rows, local_heads, width = queries.shape
    groups = cache_keys.shape[1]
    group = local_heads // groups
    shards = lax.axis_size("ctx")
    position = lax.axis_index("ctx")
    cache_frames = frame_of_slot.shape[0] * shards
    parity = position % 2
    other = 1 - parity
    keep_keys = lax.dynamic_slice_in_dim(cache_keys, parity, 1, 1)
    keep_values = lax.dynamic_slice_in_dim(cache_values, parity, 1, 1)
    keep_new_keys = lax.dynamic_slice_in_dim(new_keys, parity, 1, 1)
    keep_new_values = lax.dynamic_slice_in_dim(new_values, parity, 1, 1)
    sent = (
        lax.dynamic_slice_in_dim(cache_keys, other, 1, 1),
        lax.dynamic_slice_in_dim(cache_values, other, 1, 1),
        lax.dynamic_slice_in_dim(new_keys, other, 1, 1),
        lax.dynamic_slice_in_dim(new_values, other, 1, 1),
    )
    got_keys, got_values, got_new_keys, got_new_values = from_partner(
        (sent[0], sent[1], sent[2], sent[3]), "ctx", 0
    )
    got_frames = from_partner(frame_of_slot, "ctx", 0)
    pair_keys = jnp.concatenate([keep_keys, got_keys], axis=0)
    pair_values = jnp.concatenate([keep_values, got_values], axis=0)
    pair_frames = jnp.concatenate([frame_of_slot, got_frames], axis=0)
    lower = parity == 0
    pair_new_keys = jnp.where(
        lower,
        jnp.concatenate([keep_new_keys, got_new_keys], axis=0),
        jnp.concatenate([got_new_keys, keep_new_keys], axis=0),
    )
    pair_new_values = jnp.where(
        lower,
        jnp.concatenate([keep_new_values, got_new_values], axis=0),
        jnp.concatenate([got_new_values, keep_new_values], axis=0),
    )
    pair_start = (position - parity) * new_keys.shape[0]
    split_heads = jnp.transpose(queries.reshape(rows, groups, group, width), (1, 0, 2, 3))
    outgoing = jnp.tile(split_heads, (shards // groups, 1, 1, 1))
    everyone = lax.all_to_all(outgoing, "ctx", split_axis=0, concat_axis=0, tiled=True).reshape(
        shards * rows, group, width
    )
    my_slopes = lax.dynamic_slice_in_dim(slopes, parity * group, group)
    count = rows * shards
    acc, high, total = attend(
        everyone,
        (
            jnp.zeros((count, 1, group, width), jnp.float32),
            jnp.full((count, 1, group), -1e30, jnp.float32),
            jnp.zeros((count, 1, group), jnp.float32),
        ),
        pair_keys,
        pair_values,
        pair_frames,
        pair_new_keys,
        pair_new_values,
        my_slopes,
        pair_start,
        cache_frames,
    )
    acc, high, total = (
        lax.all_to_all(acc, "ctx", split_axis=0, concat_axis=0, tiled=True),
        lax.all_to_all(high, "ctx", split_axis=0, concat_axis=0, tiled=True),
        lax.all_to_all(total, "ctx", split_axis=0, concat_axis=0, tiled=True),
    )
    acc = acc.reshape(shards // groups, groups, rows, group, width)
    high = high.reshape(shards // groups, groups, rows, group)
    total = total.reshape(shards // groups, groups, rows, group)
    merged = jnp.transpose(combine_sources(acc, high, total), (1, 0, 2, 3))
    result = merged.astype(jnp.bfloat16).reshape(rows, local_heads * width)
    return lax.all_gather(result, "head", axis=1, tiled=True)


def on_device(*arrays):
    fresh, local, width = arrays[0].shape
    cached = arrays[1].shape[0]
    frames = arrays[5].shape[0]
    shards, heads = lax.axis_size("ctx"), lax.axis_size("head")
    whole_tiles = fresh % 16 == 0 and cached % 16 == 0 and width % 128 == 0
    pairs = shards % 2 == 0 and shards > 4 and heads % 2 == 0
    if whole_tiles and pairs and frames == 1 and (local // arrays[1].shape[1]) % PARTS == 0:
        return in_one_kernel(*arrays)
    return in_steps(*arrays)


def solution(mesh):
    return jax.shard_map(
        on_device,
        mesh=mesh,
        in_specs=(
            P("ctx", "head", None),
            P("ctx", "head", None),
            P("ctx", "head", None),
            P("ctx", "head", None),
            P("ctx", "head", None),
            P("ctx"),
            P("head"),
        ),
        out_specs=P("ctx", None),
        check_vma=False,
    )
```

```python
import functools
import math

import jax
import jax.numpy as jnp
from jax import lax
from jax.experimental import pallas as pl
from jax.experimental.pallas import tpu as pltpu
from jax.sharding import PartitionSpec as P

FRAME = 256
FRAME_BITS = FRAME.bit_length() - 1
MESH = pl.DeviceIdType.MESH
LOG2E = 1.0 / math.log(2.0)
PARTS = 4


def nt(a, b):
    return lax.dot_general(a, b, (((1,), (1,)), ((), ())), preferred_element_type=jnp.float32)


def iota(shape, dim):
    return lax.broadcasted_iota(jnp.int32, shape, dim)


def kernel(
    sizes,
    q_in,
    ck_in,
    cv_in,
    nk_in,
    nv_in,
    frame_in,
    slope_in,
    o_ref,
    q_ref,
    ck_ref,
    cv_ref,
    nk_ref,
    nv_ref,
    frame_ref,
    slope_ref,
    kv,
    qb,
    slope_rows,
    acc,
    high,
    total,
    part_out,
    part_in,
    in_sem,
    kv_up,
    kv_down,
    kv_recv,
    q_send,
    q_recv,
    p_send,
    p_recv,
    o_send,
    o_recv,
):
    cached, fresh, groups, group, width, shards, heads = sizes
    column = shards // 2
    rows = group * fresh
    cache_frames = shards
    position = lax.axis_index("ctx")
    me = lax.axis_index("head")
    side = position % 2
    place = position // 2
    across = position + 1 - 2 * side
    sibling = me + 1 - 2 * (me % 2)
    peers = [lax.rem(me + 2 * k, heads) for k in range(1, heads // 2)]
    last = column - 1
    has_up = place < last
    has_down = place > 0
    scale = LOG2E / width**0.5
    k_at = fresh
    f_at = fresh + cached
    v_at = f_at + 16
    n_at = v_at + cached

    fetches = [
        pltpu.make_async_copy(src, dst, in_sem.at[k])
        for k, (src, dst) in enumerate(
            (
                (ck_in, ck_ref),
                (nk_in, nk_ref),
                (cv_in, cv_ref),
                (nv_in, nv_ref),
                (frame_in, frame_ref),
                (q_in, q_ref),
                (slope_in, slope_ref),
            )
        )
    ]
    for fetch in fetches:
        fetch.start()

    barrier = pltpu.get_barrier_semaphore()
    pl.semaphore_signal(barrier, inc=1, device_id={"ctx": across}, device_id_type=MESH)
    for other in [sibling] + peers:
        pl.semaphore_signal(barrier, inc=1, device_id={"head": other}, device_id_type=MESH)

    @pl.when(has_up)
    def _():
        pl.semaphore_signal(barrier, inc=1, device_id={"ctx": position + 2}, device_id_type=MESH)

    @pl.when(has_down)
    def _():
        pl.semaphore_signal(barrier, inc=1, device_id={"ctx": position - 2}, device_id_type=MESH)

    pieces = ((0, v_at), (v_at, n_at + fresh))

    def slab_copy(src, g, h, to_up):
        start, stop = pieces[h]
        if not to_up:
            start, stop = max(start, k_at), min(stop, n_at)
        ref = kv.at[src, g, start:stop]
        return pltpu.make_async_remote_copy(
            src_ref=ref,
            dst_ref=ref,
            send_sem=(kv_up if to_up else kv_down).at[src, g, h],
            recv_sem=kv_recv.at[src, g, h],
            device_id={"ctx": position + 2 if to_up else position - 2},
            device_id_type=MESH,
        )

    def send_own(g, h):
        @pl.when(has_up)
        def _():
            slab_copy(place, g, h, True).start()

        @pl.when(has_down)
        def _():
            slab_copy(place, g, h, False).start()

    for fetch in fetches[:5]:
        fetch.wait()
    frame = frame_ref[0].astype(jnp.float32)
    slant = iota((cached, groups * cached), 1) - groups * iota((cached, groups * cached), 0)
    for g in range(groups):
        pick = (slant == g).astype(jnp.float32).astype(jnp.bfloat16)
        few = pick[:fresh, : groups * fresh]
        for src, at, sel, n in (
            (nk_ref, 0, few, fresh),
            (ck_ref, k_at, pick, cached),
            (cv_ref, v_at, pick, cached),
            (nv_ref, n_at, few, fresh),
        ):
            kv[place, g, at : at + n, :] = jnp.dot(
                sel, src[...], preferred_element_type=jnp.float32
            ).astype(jnp.bfloat16)
        kv[place, g, f_at:v_at, :] = jnp.full((16, width), frame, jnp.float32).astype(jnp.bfloat16)
        if g == 0:
            pl.semaphore_wait(
                barrier, 1 + heads // 2 + jnp.minimum(place, 1) + jnp.minimum(last - place, 1)
            )

        send_own(g, 0)
        if g == 0:
            send_own(g, 1)

    def q_copy(g):
        return pltpu.make_async_remote_copy(
            src_ref=qb.at[0, g],
            dst_ref=qb.at[1, g],
            send_sem=q_send.at[g],
            recv_sem=q_recv.at[g],
            device_id={"ctx": across},
            device_id_type=MESH,
        )

    for fetch in fetches[5:]:
        fetch.wait()
    local = groups * group
    slant = iota((fresh, local * fresh), 1) - local * iota((fresh, local * fresh), 0)
    for g in range(groups):
        pick = jnp.concatenate(
            [
                (slant == g * group + j).astype(jnp.float32).astype(jnp.bfloat16)
                for j in range(group)
            ],
            axis=0,
        )
        qb[0, g] = jnp.dot(pick, q_ref[...], preferred_element_type=jnp.float32).astype(jnp.bfloat16)
        q_copy(g).start()

    token = iota((1, rows), 1)
    for g in range(groups):
        row = jnp.full((1, rows), slope_ref[g * group])
        for j in range(1, group):
            row = jnp.where(token >= j * fresh, slope_ref[g * group + j], row)
        slope_rows[g] = row * LOG2E
    for j in range(group - 1, 0, -1):
        token = jnp.where(token >= j * fresh, token - j * fresh, token)

    def query_position(r):
        owner = position if r == 0 else across
        return owner * fresh + token

    def frame_of(positions):
        return (cache_frames + jnp.right_shift(positions, FRAME_BITS)).astype(jnp.float32)

    for i in range(2 * groups):
        acc[i] = jnp.zeros((width, rows), jnp.float32)
        high[i] = jnp.full((1, rows), -1e30, jnp.float32)
        total[i] = jnp.zeros((1, rows), jnp.float32)

    def attend(src, g, sides, seen):
        keys = kv[src, g, 0 if seen else k_at : f_at, :]
        values = kv[src, g, v_at : n_at + fresh if seen else n_at, :].T
        key_frame = kv[src, g, f_at:v_at, :].astype(jnp.float32)[0:1, 0:1]
        key_position = iota((fresh, 1), 0) + (2 * src + side) * fresh
        new_frame = frame_of(key_position)
        slope = slope_rows[g]
        before = [(high[2 * g + r], total[2 * g + r], acc[2 * g + r]) for r in sides]
        after = []
        for r, (top, sums, out) in zip(sides, before):
            score = nt(keys, qb[r, g]) * scale
            here = query_position(r)
            shift = slope * (key_frame - frame_of(here))
            old = score[fresh:] if seen else score
            now = jnp.maximum(top, jnp.max(old, axis=0, keepdims=True) + shift)
            if seen:
                new = score[:fresh] + slope * (new_frame - frame_of(here))
                new = jnp.where(key_position <= here, new, -1e30)
                now = jnp.maximum(now, jnp.max(new, axis=0, keepdims=True))
            corr = jnp.exp2(top - now)
            old = jnp.exp2(old + (shift - now))
            fresh_sum = jnp.sum(old, axis=0, keepdims=True)
            weight = old.astype(jnp.bfloat16)
            if seen:
                new = jnp.exp2(new - now)
                fresh_sum = fresh_sum + jnp.sum(new, axis=0, keepdims=True)
                weight = jnp.concatenate([weight, new.astype(jnp.bfloat16)], axis=0)
            out = out * corr + jnp.dot(values, weight, preferred_element_type=jnp.float32)
            after.append((now, sums * corr + fresh_sum, out))
        for r, (now, sums, out) in zip(sides, after):
            high[2 * g + r] = now
            total[2 * g + r] = sums
            acc[2 * g + r] = out

    def pass_on(apart, g):
        low = place - apart
        top = place + apart

        @pl.when(low >= 0)
        def _():
            for h in range(2):
                slab_copy(low, g, h, True).wait_recv()

                @pl.when(has_up)
                def _():
                    slab_copy(low, g, h, True).start()

        @pl.when(top <= last)
        def _():
            for h in range(2):
                slab_copy(top, g, h, False).wait_recv()

                @pl.when(has_down)
                def _():
                    slab_copy(top, g, h, False).start()

    def attend_pair(apart, g, sides=(1, 0)):
        low = place - apart
        top = place + apart

        @pl.when(low >= 0)
        def _():
            attend(low, g, sides, True)

        @pl.when(top <= last)
        def _():
            attend(top, g, sides, False)

    part_rows = rows // PARTS
    part_heads = group // PARTS

    def p_copy(i):
        return pltpu.make_async_remote_copy(
            src_ref=part_out.at[i],
            dst_ref=part_in.at[i],
            send_sem=p_send.at[i],
            recv_sem=p_recv.at[i],
            device_id={"ctx": across},
            device_id_type=MESH,
        )

    def finish(g):
        sub = iota((16, part_rows), 0)
        for c in range(PARTS):
            i = g * PARTS + c
            cols = slice(c * part_rows, (c + 1) * part_rows)
            sums = total[2 * g + 1, :, cols]
            part_out[i, 0:width, :] = (acc[2 * g + 1, :, cols] * (1.0 / sums)).astype(jnp.bfloat16)
            lse = high[2 * g + 1, :, cols] + jnp.log(sums) * LOG2E
            one = lse.astype(jnp.bfloat16).astype(jnp.float32)
            two = (lse - one).astype(jnp.bfloat16).astype(jnp.float32)
            three = lse - one - two
            stats = jnp.where(sub == 0, one, jnp.where(sub == 1, two, three))
            part_out[i, width : width + 16, :] = stats.astype(jnp.bfloat16)
            p_copy(i).start()

    def block_of(owner, i):
        at = (owner * groups * PARTS + i) * part_heads * width
        return o_ref.at[:, pl.ds(pl.multiple_of(at, part_heads * width), part_heads * width)]

    def o_copy(owner, i, slot, target):
        return pltpu.make_async_remote_copy(
            src_ref=block_of(owner, i),
            dst_ref=block_of(owner, i),
            send_sem=o_send.at[slot, i],
            recv_sem=o_recv.at[owner, i],
            device_id={"head": target},
            device_id_type=MESH,
        )

    def combine(i):
        g, c = divmod(i, PARTS)
        cols = slice(c * part_rows, (c + 1) * part_rows)
        sums = total[2 * g, :, cols]
        mine = high[2 * g, :, cols] + jnp.log(sums) * LOG2E
        p_copy(i).wait_recv()
        stats = part_in[i, width : width + 16, :].astype(jnp.float32)
        theirs = stats[0:1] + stats[1:2] + stats[2:3]
        top = jnp.maximum(mine, theirs)
        a = jnp.exp2(mine - top)
        b = jnp.exp2(theirs - top)
        both = a + b
        out = acc[2 * g, :, cols] * (a / (sums * both)) + part_in[i, 0:width, :].astype(
            jnp.float32
        ) * (b / both)
        out = out.T
        at = (me * groups * PARTS + i) * part_heads * width
        for j in range(part_heads):
            spot = pl.multiple_of(at + j * width, width)
            o_ref[:, pl.ds(spot, width)] = out[j * fresh : (j + 1) * fresh].astype(jnp.bfloat16)
        for k, peer in enumerate(peers):
            o_copy(me, i, 1 + k, peer).start()
        o_copy(me, i, 0, sibling).start()

    def forward(i):
        for k, peer in enumerate(peers):
            o_copy(peer, i, 0, sibling).wait_recv()
            o_copy(peer, i, 1 + len(peers) + k, sibling).start()

    def body(k, carry):
        g = jnp.where(k == 0, 0, 1 - k % 2)
        apart = jnp.where(k == 0, 1, jnp.where(k % 2 == 1, (k + 3) // 2, k // 2))
        pass_on(apart, g)

        @pl.when(k == 0)
        def _():
            send_own(1, 1)

        @pl.when(apart == 1)
        def _():
            q_copy(g).wait_recv()
            attend(place, g, (1,), True)

        attend_pair(apart, g)
        return carry

    count = groups * PARTS
    for g in range(groups):
        attend(place, g, (0,), True)
    lax.fori_loop(0, 2 * last - 3, body, 0)
    pass_on(last, 0)
    attend_pair(last, 0, (1,))
    finish(0)
    attend_pair(last, 0, (0,))
    pass_on(last - 1, 1)
    attend_pair(last - 1, 1)
    for c in range(PARTS):
        combine(c)
    pass_on(last, 1)
    attend_pair(last, 1, (1,))
    finish(1)
    attend_pair(last, 1, (0,))
    for c in range(PARTS):
        combine(count - PARTS + c)
        for g in range(groups - 1):
            forward(g * PARTS + c)
    for i in range(count - PARTS, count):
        forward(i)
    for i in range(count):
        o_copy(sibling, i, 0, sibling).wait_recv()
        for peer in peers:
            far = peer + 1 - 2 * (peer % 2)
            o_copy(far, i, 0, sibling).wait_recv()

    for g in range(groups):
        for src in range(column):

            @pl.when(jnp.logical_and(has_up, src <= place))
            def _():
                for h in range(2):
                    slab_copy(src, g, h, True).wait_send()

            @pl.when(jnp.logical_and(has_down, src >= place))
            def _():
                for h in range(2):
                    slab_copy(src, g, h, False).wait_send()

        q_copy(g).wait_send()
    for i in range(count):
        p_copy(i).wait_send()
        o_copy(me, i, 0, sibling).wait_send()
        for k, peer in enumerate(peers):
            o_copy(me, i, 1 + k, peer).wait_send()
            o_copy(peer, i, 1 + len(peers) + k, sibling).wait_send()


def in_one_kernel(queries, cache_keys, cache_values, new_keys, new_values, frame_of_slot, slopes):
    fresh, local, width = queries.shape
    cached, groups, _ = cache_keys.shape
    group = local // groups
    shards = lax.axis_size("ctx")
    heads = lax.axis_size("head")
    column = shards // 2
    rows = group * fresh
    slab = 2 * (cached + fresh) + 16
    count = groups * PARTS
    vmem = pl.BlockSpec(memory_space=pltpu.VMEM)
    dma = pltpu.SemaphoreType.DMA
    sizes = (cached, fresh, groups, group, width, shards, heads)
    return pl.pallas_call(
        functools.partial(kernel, sizes),
        out_shape=pltpu.VMEM((fresh, heads * local * width), jnp.bfloat16),
        in_specs=[pl.BlockSpec(memory_space=pl.ANY)] * 7,
        out_specs=vmem,
        scratch_shapes=[
            pltpu.VMEM((fresh * local, width), jnp.bfloat16),
            pltpu.VMEM((cached * groups, width), jnp.bfloat16),
            pltpu.VMEM((cached * groups, width), jnp.bfloat16),
            pltpu.VMEM((fresh * groups, width), jnp.bfloat16),
            pltpu.VMEM((fresh * groups, width), jnp.bfloat16),
            pltpu.SMEM(frame_of_slot.shape, jnp.int32),
            pltpu.SMEM(slopes.shape, jnp.float32),
            pltpu.VMEM((column, groups, slab, width), jnp.bfloat16),
            pltpu.VMEM((2, groups, rows, width), jnp.bfloat16),
            pltpu.VMEM((groups, 1, rows), jnp.float32),
            pltpu.VMEM((2 * groups, width, rows), jnp.float32),
            pltpu.VMEM((2 * groups, 1, rows), jnp.float32),
            pltpu.VMEM((2 * groups, 1, rows), jnp.float32),
            pltpu.VMEM((count, width + 16, rows // PARTS), jnp.bfloat16),
            pltpu.VMEM((count, width + 16, rows // PARTS), jnp.bfloat16),
            dma((7,)),
            dma((column, groups, 2)),
            dma((column, groups, 2)),
            dma((column, groups, 2)),
            dma((groups,)),
            dma((groups,)),
            dma((count,)),
            dma((count,)),
            dma((heads - 1, count)),
            dma((heads, count)),
        ],
        compiler_params=pltpu.CompilerParams(
            collective_id=0, has_side_effects=True, vmem_limit_bytes=62 * 1024 * 1024
        ),
        name="attend_over_slice",
    )(
        queries.reshape(fresh * local, width),
        cache_keys.reshape(cached * groups, width),
        cache_values.reshape(cached * groups, width),
        new_keys.reshape(fresh * groups, width),
        new_values.reshape(fresh * groups, width),
        frame_of_slot,
        slopes,
    )


def from_partner(value, axis, apart):
    return lax.ppermute(value, axis, [(i, i ^ 1 << apart) for i in range(lax.axis_size(axis))])


def update(state, score, values):
    acc, high, total = state
    new_high = jnp.maximum(high, jnp.max(score, axis=-1))
    corr = jnp.exp(high - new_high)
    expo = jnp.exp(score - new_high[..., None])
    total = total * corr + jnp.sum(expo, axis=-1)
    weight = expo.astype(jnp.bfloat16)
    acc = acc * corr[..., None] + jnp.einsum(
        "rgqk,kgd->rgqd", weight, values, preferred_element_type=jnp.float32
    )
    return (acc, new_high, total)


def attend(
    q_rows,
    state,
    cache_keys,
    cache_values,
    key_frames,
    new_keys,
    new_values,
    slopes,
    key_start,
    cache_frames,
):
    rows, local_heads, width = q_rows.shape
    groups = cache_keys.shape[1]
    group = local_heads // groups
    scale = 1.0 / width**0.5
    query = q_rows.reshape(rows, groups, group, width)
    qpos = jnp.arange(rows, dtype=jnp.int32)
    qframe = (cache_frames + qpos // FRAME).astype(jnp.float32)
    slope = slopes.reshape(groups, group)
    frames = key_frames.shape[0]
    kblocks = cache_keys.reshape(frames, FRAME, groups, width)
    vblocks = cache_values.reshape(frames, FRAME, groups, width)

    def scan_step(carry, items):
        kb, vb, fb = items
        score = jnp.einsum("rgqd,kgd->rgqk", query, kb, preferred_element_type=jnp.float32) * scale
        distance = qframe - fb.astype(jnp.float32)
        score = score - slope[None, :, :, None] * distance[:, None, None, None]
        return (update(carry, score, vb), None)

    state, _ = lax.scan(scan_step, state, (kblocks, vblocks, key_frames))
    kpos = key_start + jnp.arange(new_keys.shape[0], dtype=jnp.int32)
    kframe = (cache_frames + kpos // FRAME).astype(jnp.float32)
    score = (
        jnp.einsum("rgqd,kgd->rgqk", query, new_keys, preferred_element_type=jnp.float32) * scale
    )
    score = score - slope[None, :, :, None] * (qframe[:, None] - kframe[None, :])[:, None, None, :]
    visible = kpos[None, :] <= qpos[:, None]
    score = jnp.where(visible[:, None, None, :], score, -1e30)
    return update(state, score, new_values)


def combine_sources(acc, high, total):
    top = jnp.max(high, axis=0)
    scaling = jnp.exp(high - top[None])
    return jnp.sum(acc * scaling[..., None], axis=0) / jnp.sum(total * scaling, axis=0)[..., None]


def in_steps(queries, cache_keys, cache_values, new_keys, new_values, frame_of_slot, slopes):
    rows, local_heads, width = queries.shape
    groups = cache_keys.shape[1]
    group = local_heads // groups
    shards = lax.axis_size("ctx")
    position = lax.axis_index("ctx")
    cache_frames = frame_of_slot.shape[0] * shards
    parity = position % 2
    other = 1 - parity
    keep_keys = lax.dynamic_slice_in_dim(cache_keys, parity, 1, 1)
    keep_values = lax.dynamic_slice_in_dim(cache_values, parity, 1, 1)
    keep_new_keys = lax.dynamic_slice_in_dim(new_keys, parity, 1, 1)
    keep_new_values = lax.dynamic_slice_in_dim(new_values, parity, 1, 1)
    sent = (
        lax.dynamic_slice_in_dim(cache_keys, other, 1, 1),
        lax.dynamic_slice_in_dim(cache_values, other, 1, 1),
        lax.dynamic_slice_in_dim(new_keys, other, 1, 1),
        lax.dynamic_slice_in_dim(new_values, other, 1, 1),
    )
    got_keys, got_values, got_new_keys, got_new_values = from_partner(
        (sent[0], sent[1], sent[2], sent[3]), "ctx", 0
    )
    got_frames = from_partner(frame_of_slot, "ctx", 0)
    pair_keys = jnp.concatenate([keep_keys, got_keys], axis=0)
    pair_values = jnp.concatenate([keep_values, got_values], axis=0)
    pair_frames = jnp.concatenate([frame_of_slot, got_frames], axis=0)
    lower = parity == 0
    pair_new_keys = jnp.where(
        lower,
        jnp.concatenate([keep_new_keys, got_new_keys], axis=0),
        jnp.concatenate([got_new_keys, keep_new_keys], axis=0),
    )
    pair_new_values = jnp.where(
        lower,
        jnp.concatenate([keep_new_values, got_new_values], axis=0),
        jnp.concatenate([got_new_values, keep_new_values], axis=0),
    )
    pair_start = (position - parity) * new_keys.shape[0]
    split_heads = jnp.transpose(queries.reshape(rows, groups, group, width), (1, 0, 2, 3))
    outgoing = jnp.tile(split_heads, (shards // groups, 1, 1, 1))
    everyone = lax.all_to_all(outgoing, "ctx", split_axis=0, concat_axis=0, tiled=True).reshape(
        shards * rows, group, width
    )
    my_slopes = lax.dynamic_slice_in_dim(slopes, parity * group, group)
    count = rows * shards
    acc, high, total = attend(
        everyone,
        (
            jnp.zeros((count, 1, group, width), jnp.float32),
            jnp.full((count, 1, group), -1e30, jnp.float32),
            jnp.zeros((count, 1, group), jnp.float32),
        ),
        pair_keys,
        pair_values,
        pair_frames,
        pair_new_keys,
        pair_new_values,
        my_slopes,
        pair_start,
        cache_frames,
    )
    acc, high, total = (
        lax.all_to_all(acc, "ctx", split_axis=0, concat_axis=0, tiled=True),
        lax.all_to_all(high, "ctx", split_axis=0, concat_axis=0, tiled=True),
        lax.all_to_all(total, "ctx", split_axis=0, concat_axis=0, tiled=True),
    )
    acc = acc.reshape(shards // groups, groups, rows, group, width)
    high = high.reshape(shards // groups, groups, rows, group)
    total = total.reshape(shards // groups, groups, rows, group)
    merged = jnp.transpose(combine_sources(acc, high, total), (1, 0, 2, 3))
    result = merged.astype(jnp.bfloat16).reshape(rows, local_heads * width)
    return lax.all_gather(result, "head", axis=1, tiled=True)


def on_device(*arrays):
    fresh, local, width = arrays[0].shape
    cached = arrays[1].shape[0]
    frames = arrays[5].shape[0]
    shards, heads = lax.axis_size("ctx"), lax.axis_size("head")
    whole_tiles = fresh % 16 == 0 and cached % 16 == 0 and width % 128 == 0
    pairs = shards % 2 == 0 and shards > 6 and heads % 2 == 0 and arrays[1].shape[1] == 2
    if whole_tiles and pairs and frames == 1 and (local // arrays[1].shape[1]) % PARTS == 0:
        return in_one_kernel(*arrays)
    return in_steps(*arrays)


def solution(mesh):
    return jax.shard_map(
        on_device,
        mesh=mesh,
        in_specs=(
            P("ctx", "head", None),
            P("ctx", "head", None),
            P("ctx", "head", None),
            P("ctx", "head", None),
            P("ctx", "head", None),
            P("ctx"),
            P("head"),
        ),
        out_specs=P("ctx", None),
        check_vma=False,
    )
```

```python
import functools
import math

import jax
import jax.numpy as jnp
from jax import lax
from jax.experimental import pallas as pl
from jax.experimental.pallas import tpu as pltpu
from jax.sharding import PartitionSpec as P

FRAME = 256
FRAME_BITS = FRAME.bit_length() - 1
MESH = pl.DeviceIdType.MESH
LOG2E = 1.0 / math.log(2.0)
PARTS = 4


def nt(a, b):
    return lax.dot_general(a, b, (((1,), (1,)), ((), ())), preferred_element_type=jnp.float32)


def iota(shape, dim):
    return lax.broadcasted_iota(jnp.int32, shape, dim)


def kernel(
    sizes,
    q_in,
    ck_in,
    cv_in,
    nk_in,
    nv_in,
    frame_in,
    slope_in,
    o_ref,
    q_ref,
    ck_ref,
    cv_ref,
    nk_ref,
    nv_ref,
    frame_ref,
    slope_ref,
    kv,
    qb,
    slope_rows,
    acc,
    high,
    total,
    part_out,
    part_in,
    in_sem,
    kv_up,
    kv_down,
    kv_recv,
    q_send,
    q_recv,
    p_send,
    p_recv,
    o_send,
    o_recv,
):
    cached, fresh, groups, group, width, shards, heads = sizes
    column = shards // 2
    rows = group * fresh
    cache_frames = shards
    position = lax.axis_index("ctx")
    me = lax.axis_index("head")
    side = position % 2
    place = position // 2
    across = position + 1 - 2 * side
    sibling = me + 1 - 2 * (me % 2)
    peers = [lax.rem(me + 2 * k, heads) for k in range(1, heads // 2)]
    last = column - 1
    has_up = place < last
    has_down = place > 0
    scale = LOG2E / width**0.5
    k_at = fresh
    f_at = fresh + cached
    v_at = f_at + 16
    n_at = v_at + cached

    fetches = [
        pltpu.make_async_copy(src, dst, in_sem.at[k])
        for k, (src, dst) in enumerate(
            (
                (ck_in, ck_ref),
                (nk_in, nk_ref),
                (cv_in, cv_ref),
                (nv_in, nv_ref),
                (frame_in, frame_ref),
                (q_in, q_ref),
                (slope_in, slope_ref),
            )
        )
    ]
    for fetch in fetches:
        fetch.start()

    barrier = pltpu.get_barrier_semaphore()
    pl.semaphore_signal(barrier, inc=1, device_id={"ctx": across}, device_id_type=MESH)
    for other in [sibling] + peers:
        pl.semaphore_signal(barrier, inc=1, device_id={"head": other}, device_id_type=MESH)

    @pl.when(has_up)
    def _():
        pl.semaphore_signal(barrier, inc=1, device_id={"ctx": position + 2}, device_id_type=MESH)

    @pl.when(has_down)
    def _():
        pl.semaphore_signal(barrier, inc=1, device_id={"ctx": position - 2}, device_id_type=MESH)

    pieces = ((0, v_at), (v_at, n_at + fresh))

    def slab_copy(src, g, h, to_up):
        start, stop = pieces[h]
        if not to_up:
            start, stop = max(start, k_at), min(stop, n_at)
        ref = kv.at[src, g, start:stop]
        return pltpu.make_async_remote_copy(
            src_ref=ref,
            dst_ref=ref,
            send_sem=(kv_up if to_up else kv_down).at[src, g, h],
            recv_sem=kv_recv.at[src, g, h],
            device_id={"ctx": position + 2 if to_up else position - 2},
            device_id_type=MESH,
        )

    def send_own(g, h):
        @pl.when(has_up)
        def _():
            slab_copy(place, g, h, True).start()

        @pl.when(has_down)
        def _():
            slab_copy(place, g, h, False).start()

    slant = iota((cached, groups * cached), 1) - groups * iota((cached, groups * cached), 0)
    picks = [(slant == g).astype(jnp.float32).astype(jnp.bfloat16) for g in range(groups)]
    for fetch in fetches[:5]:
        fetch.wait()
    frame = frame_ref[0].astype(jnp.float32)
    for g in range(groups):
        pick = picks[g]
        few = pick[:fresh, : groups * fresh]
        for src, at, sel, n in (
            (nk_ref, 0, few, fresh),
            (ck_ref, k_at, pick, cached),
            (cv_ref, v_at, pick, cached),
            (nv_ref, n_at, few, fresh),
        ):
            kv[place, g, at : at + n, :] = jnp.dot(
                sel, src[...], preferred_element_type=jnp.float32
            ).astype(jnp.bfloat16)
        kv[place, g, f_at:v_at, :] = jnp.full((16, width), frame, jnp.float32).astype(jnp.bfloat16)
        if g == 0:
            pl.semaphore_wait(
                barrier, 1 + heads // 2 + jnp.minimum(place, 1) + jnp.minimum(last - place, 1)
            )

        send_own(g, 0)
        if g == 0:
            send_own(g, 1)

    def q_copy(g):
        return pltpu.make_async_remote_copy(
            src_ref=qb.at[0, g],
            dst_ref=qb.at[1, g],
            send_sem=q_send.at[g],
            recv_sem=q_recv.at[g],
            device_id={"ctx": across},
            device_id_type=MESH,
        )

    for fetch in fetches[5:]:
        fetch.wait()
    local = groups * group
    slant = iota((fresh, local * fresh), 1) - local * iota((fresh, local * fresh), 0)
    for g in range(groups):
        pick = jnp.concatenate(
            [
                (slant == g * group + j).astype(jnp.float32).astype(jnp.bfloat16)
                for j in range(group)
            ],
            axis=0,
        )
        qb[0, g] = jnp.dot(pick, q_ref[...], preferred_element_type=jnp.float32).astype(jnp.bfloat16)
        q_copy(g).start()

    token = iota((1, rows), 1)
    for g in range(groups):
        row = jnp.full((1, rows), slope_ref[g * group])
        for j in range(1, group):
            row = jnp.where(token >= j * fresh, slope_ref[g * group + j], row)
        slope_rows[g] = row * LOG2E
    for j in range(group - 1, 0, -1):
        token = jnp.where(token >= j * fresh, token - j * fresh, token)

    def query_position(r):
        owner = position if r == 0 else across
        return owner * fresh + token

    def frame_of(positions):
        return (cache_frames + jnp.right_shift(positions, FRAME_BITS)).astype(jnp.float32)

    for i in range(2 * groups):
        acc[i] = jnp.zeros((width, rows), jnp.float32)
        high[i] = jnp.full((1, rows), -1e30, jnp.float32)
        total[i] = jnp.zeros((1, rows), jnp.float32)

    def attend(src, g, sides, seen, cols=slice(None)):
        keys = kv[src, g, 0 if seen else k_at : f_at, :]
        values = kv[src, g, v_at : n_at + fresh if seen else n_at, :].T
        key_frame = kv[src, g, f_at:v_at, :].astype(jnp.float32)[0:1, 0:1]
        key_position = iota((fresh, 1), 0) + (2 * src + side) * fresh
        new_frame = frame_of(key_position)
        slope = slope_rows[g, :, cols]
        before = [
            (high[2 * g + r, :, cols], total[2 * g + r, :, cols], acc[2 * g + r, :, cols])
            for r in sides
        ]
        after = []
        for r, (top, sums, out) in zip(sides, before):
            score = nt(keys, qb[r, g, cols]) * scale
            here = query_position(r)[:, cols]
            shift = slope * (key_frame - frame_of(here))
            old = score[fresh:] if seen else score
            now = jnp.maximum(top, jnp.max(old, axis=0, keepdims=True) + shift)
            if seen:
                new = score[:fresh] + slope * (new_frame - frame_of(here))
                new = jnp.where(key_position <= here, new, -1e30)
                now = jnp.maximum(now, jnp.max(new, axis=0, keepdims=True))
            corr = jnp.exp2(top - now)
            old = jnp.exp2(old + (shift - now))
            fresh_sum = jnp.sum(old, axis=0, keepdims=True)
            weight = old.astype(jnp.bfloat16)
            if seen:
                new = jnp.exp2(new - now)
                fresh_sum = fresh_sum + jnp.sum(new, axis=0, keepdims=True)
                weight = jnp.concatenate([weight, new.astype(jnp.bfloat16)], axis=0)
            out = out * corr + jnp.dot(values, weight, preferred_element_type=jnp.float32)
            after.append((now, sums * corr + fresh_sum, out))
        for r, (now, sums, out) in zip(sides, after):
            high[2 * g + r, :, cols] = now
            total[2 * g + r, :, cols] = sums
            acc[2 * g + r, :, cols] = out

    def pass_on(apart, g):
        low = place - apart
        top = place + apart

        @pl.when(low >= 0)
        def _():
            for h in range(2):
                slab_copy(low, g, h, True).wait_recv()

                @pl.when(has_up)
                def _():
                    slab_copy(low, g, h, True).start()

        @pl.when(top <= last)
        def _():
            for h in range(2):
                slab_copy(top, g, h, False).wait_recv()

                @pl.when(has_down)
                def _():
                    slab_copy(top, g, h, False).start()

    def attend_pair(apart, g, sides=(1, 0), cols=slice(None)):
        low = place - apart
        top = place + apart

        @pl.when(low >= 0)
        def _():
            attend(low, g, sides, True, cols)

        @pl.when(top <= last)
        def _():
            attend(top, g, sides, False, cols)

    part_rows = rows // PARTS
    part_heads = group // PARTS

    def p_copy(i):
        return pltpu.make_async_remote_copy(
            src_ref=part_out.at[i],
            dst_ref=part_in.at[i],
            send_sem=p_send.at[i],
            recv_sem=p_recv.at[i],
            device_id={"ctx": across},
            device_id_type=MESH,
        )

    def finish(g, parts=range(PARTS)):
        sub = iota((16, part_rows), 0)
        for c in parts:
            i = g * PARTS + c
            cols = slice(c * part_rows, (c + 1) * part_rows)
            sums = total[2 * g + 1, :, cols]
            part_out[i, 0:width, :] = (acc[2 * g + 1, :, cols] * (1.0 / sums)).astype(jnp.bfloat16)
            lse = high[2 * g + 1, :, cols] + jnp.log(sums) * LOG2E
            one = lse.astype(jnp.bfloat16).astype(jnp.float32)
            two = (lse - one).astype(jnp.bfloat16).astype(jnp.float32)
            three = lse - one - two
            stats = jnp.where(sub == 0, one, jnp.where(sub == 1, two, three))
            part_out[i, width : width + 16, :] = stats.astype(jnp.bfloat16)
            p_copy(i).start()

    def block_of(owner, i):
        at = (owner * groups * PARTS + i) * part_heads * width
        return o_ref.at[:, pl.ds(pl.multiple_of(at, part_heads * width), part_heads * width)]

    def o_copy(owner, i, slot, target):
        return pltpu.make_async_remote_copy(
            src_ref=block_of(owner, i),
            dst_ref=block_of(owner, i),
            send_sem=o_send.at[slot, i],
            recv_sem=o_recv.at[owner, i],
            device_id={"head": target},
            device_id_type=MESH,
        )

    def combine(i):
        g, c = divmod(i, PARTS)
        cols = slice(c * part_rows, (c + 1) * part_rows)
        sums = total[2 * g, :, cols]
        mine = high[2 * g, :, cols] + jnp.log(sums) * LOG2E
        p_copy(i).wait_recv()
        stats = part_in[i, width : width + 16, :].astype(jnp.float32)
        theirs = stats[0:1] + stats[1:2] + stats[2:3]
        top = jnp.maximum(mine, theirs)
        a = jnp.exp2(mine - top)
        b = jnp.exp2(theirs - top)
        both = a + b
        out = acc[2 * g, :, cols] * (a / (sums * both)) + part_in[i, 0:width, :].astype(
            jnp.float32
        ) * (b / both)
        out = out.T
        at = (me * groups * PARTS + i) * part_heads * width
        for j in range(part_heads):
            spot = pl.multiple_of(at + j * width, width)
            o_ref[:, pl.ds(spot, width)] = out[j * fresh : (j + 1) * fresh].astype(jnp.bfloat16)
        for k, peer in enumerate(peers):
            o_copy(me, i, 1 + k, peer).start()
        o_copy(me, i, 0, sibling).start()

    def forward(i):
        for k, peer in enumerate(peers):
            o_copy(peer, i, 0, sibling).wait_recv()
            o_copy(peer, i, 1 + len(peers) + k, sibling).start()

    def body(k, carry):
        g = jnp.where(k == 0, 0, 1 - k % 2)
        apart = jnp.where(k == 0, 1, jnp.where(k % 2 == 1, (k + 3) // 2, k // 2))
        pass_on(apart, g)

        @pl.when(k == 0)
        def _():
            send_own(1, 1)

        @pl.when(apart == 1)
        def _():
            q_copy(g).wait_recv()
            attend(place, g, (1,), True)

        attend_pair(apart, g)
        return carry

    count = groups * PARTS
    for g in range(groups):
        attend(place, g, (0,), True)
    lax.fori_loop(0, 2 * last - 3, body, 0)
    pass_on(last, 0)
    attend_pair(last, 0, (1,))
    finish(0)
    attend_pair(last, 0, (0,))
    pass_on(last - 1, 1)
    attend_pair(last - 1, 1)
    for c in range(PARTS):
        combine(c)
    pass_on(last, 1)
    half = PARTS // 2
    for c in (0, half):
        attend_pair(last, 1, (1,), slice(c * part_rows, (c + half) * part_rows))
        finish(1, range(c, c + half))
    attend_pair(last, 1, (0,))
    for c in range(PARTS):
        combine(count - PARTS + c)
        for g in range(groups - 1):
            forward(g * PARTS + c)
    for i in range(count - PARTS, count):
        forward(i)
    for i in range(count):
        o_copy(sibling, i, 0, sibling).wait_recv()
        for peer in peers:
            far = peer + 1 - 2 * (peer % 2)
            o_copy(far, i, 0, sibling).wait_recv()

    for g in range(groups):
        for src in range(column):

            @pl.when(jnp.logical_and(has_up, src <= place))
            def _():
                for h in range(2):
                    slab_copy(src, g, h, True).wait_send()

            @pl.when(jnp.logical_and(has_down, src >= place))
            def _():
                for h in range(2):
                    slab_copy(src, g, h, False).wait_send()

        q_copy(g).wait_send()
    for i in range(count):
        p_copy(i).wait_send()
        o_copy(me, i, 0, sibling).wait_send()
        for k, peer in enumerate(peers):
            o_copy(me, i, 1 + k, peer).wait_send()
            o_copy(peer, i, 1 + len(peers) + k, sibling).wait_send()


def in_one_kernel(queries, cache_keys, cache_values, new_keys, new_values, frame_of_slot, slopes):
    fresh, local, width = queries.shape
    cached, groups, _ = cache_keys.shape
    group = local // groups
    shards = lax.axis_size("ctx")
    heads = lax.axis_size("head")
    column = shards // 2
    rows = group * fresh
    slab = 2 * (cached + fresh) + 16
    count = groups * PARTS
    vmem = pl.BlockSpec(memory_space=pltpu.VMEM)
    dma = pltpu.SemaphoreType.DMA
    sizes = (cached, fresh, groups, group, width, shards, heads)
    return pl.pallas_call(
        functools.partial(kernel, sizes),
        out_shape=pltpu.VMEM((fresh, heads * local * width), jnp.bfloat16),
        in_specs=[pl.BlockSpec(memory_space=pl.ANY)] * 7,
        out_specs=vmem,
        scratch_shapes=[
            pltpu.VMEM((fresh * local, width), jnp.bfloat16),
            pltpu.VMEM((cached * groups, width), jnp.bfloat16),
            pltpu.VMEM((cached * groups, width), jnp.bfloat16),
            pltpu.VMEM((fresh * groups, width), jnp.bfloat16),
            pltpu.VMEM((fresh * groups, width), jnp.bfloat16),
            pltpu.SMEM(frame_of_slot.shape, jnp.int32),
            pltpu.SMEM(slopes.shape, jnp.float32),
            pltpu.VMEM((column, groups, slab, width), jnp.bfloat16),
            pltpu.VMEM((2, groups, rows, width), jnp.bfloat16),
            pltpu.VMEM((groups, 1, rows), jnp.float32),
            pltpu.VMEM((2 * groups, width, rows), jnp.float32),
            pltpu.VMEM((2 * groups, 1, rows), jnp.float32),
            pltpu.VMEM((2 * groups, 1, rows), jnp.float32),
            pltpu.VMEM((count, width + 16, rows // PARTS), jnp.bfloat16),
            pltpu.VMEM((count, width + 16, rows // PARTS), jnp.bfloat16),
            dma((7,)),
            dma((column, groups, 2)),
            dma((column, groups, 2)),
            dma((column, groups, 2)),
            dma((groups,)),
            dma((groups,)),
            dma((count,)),
            dma((count,)),
            dma((heads - 1, count)),
            dma((heads, count)),
        ],
        compiler_params=pltpu.CompilerParams(
            collective_id=0, has_side_effects=True, vmem_limit_bytes=62 * 1024 * 1024
        ),
        name="attend_over_slice",
    )(
        queries.reshape(fresh * local, width),
        cache_keys.reshape(cached * groups, width),
        cache_values.reshape(cached * groups, width),
        new_keys.reshape(fresh * groups, width),
        new_values.reshape(fresh * groups, width),
        frame_of_slot,
        slopes,
    )


def from_partner(value, axis, apart):
    return lax.ppermute(value, axis, [(i, i ^ 1 << apart) for i in range(lax.axis_size(axis))])


def update(state, score, values):
    acc, high, total = state
    new_high = jnp.maximum(high, jnp.max(score, axis=-1))
    corr = jnp.exp(high - new_high)
    expo = jnp.exp(score - new_high[..., None])
    total = total * corr + jnp.sum(expo, axis=-1)
    weight = expo.astype(jnp.bfloat16)
    acc = acc * corr[..., None] + jnp.einsum(
        "rgqk,kgd->rgqd", weight, values, preferred_element_type=jnp.float32
    )
    return (acc, new_high, total)


def attend(
    q_rows,
    state,
    cache_keys,
    cache_values,
    key_frames,
    new_keys,
    new_values,
    slopes,
    key_start,
    cache_frames,
):
    rows, local_heads, width = q_rows.shape
    groups = cache_keys.shape[1]
    group = local_heads // groups
    scale = 1.0 / width**0.5
    query = q_rows.reshape(rows, groups, group, width)
    qpos = jnp.arange(rows, dtype=jnp.int32)
    qframe = (cache_frames + qpos // FRAME).astype(jnp.float32)
    slope = slopes.reshape(groups, group)
    frames = key_frames.shape[0]
    kblocks = cache_keys.reshape(frames, FRAME, groups, width)
    vblocks = cache_values.reshape(frames, FRAME, groups, width)

    def scan_step(carry, items):
        kb, vb, fb = items
        score = jnp.einsum("rgqd,kgd->rgqk", query, kb, preferred_element_type=jnp.float32) * scale
        distance = qframe - fb.astype(jnp.float32)
        score = score - slope[None, :, :, None] * distance[:, None, None, None]
        return (update(carry, score, vb), None)

    state, _ = lax.scan(scan_step, state, (kblocks, vblocks, key_frames))
    kpos = key_start + jnp.arange(new_keys.shape[0], dtype=jnp.int32)
    kframe = (cache_frames + kpos // FRAME).astype(jnp.float32)
    score = (
        jnp.einsum("rgqd,kgd->rgqk", query, new_keys, preferred_element_type=jnp.float32) * scale
    )
    score = score - slope[None, :, :, None] * (qframe[:, None] - kframe[None, :])[:, None, None, :]
    visible = kpos[None, :] <= qpos[:, None]
    score = jnp.where(visible[:, None, None, :], score, -1e30)
    return update(state, score, new_values)


def combine_sources(acc, high, total):
    top = jnp.max(high, axis=0)
    scaling = jnp.exp(high - top[None])
    return jnp.sum(acc * scaling[..., None], axis=0) / jnp.sum(total * scaling, axis=0)[..., None]


def in_steps(queries, cache_keys, cache_values, new_keys, new_values, frame_of_slot, slopes):
    rows, local_heads, width = queries.shape
    groups = cache_keys.shape[1]
    group = local_heads // groups
    shards = lax.axis_size("ctx")
    position = lax.axis_index("ctx")
    cache_frames = frame_of_slot.shape[0] * shards
    parity = position % 2
    other = 1 - parity
    keep_keys = lax.dynamic_slice_in_dim(cache_keys, parity, 1, 1)
    keep_values = lax.dynamic_slice_in_dim(cache_values, parity, 1, 1)
    keep_new_keys = lax.dynamic_slice_in_dim(new_keys, parity, 1, 1)
    keep_new_values = lax.dynamic_slice_in_dim(new_values, parity, 1, 1)
    sent = (
        lax.dynamic_slice_in_dim(cache_keys, other, 1, 1),
        lax.dynamic_slice_in_dim(cache_values, other, 1, 1),
        lax.dynamic_slice_in_dim(new_keys, other, 1, 1),
        lax.dynamic_slice_in_dim(new_values, other, 1, 1),
    )
    got_keys, got_values, got_new_keys, got_new_values = from_partner(
        (sent[0], sent[1], sent[2], sent[3]), "ctx", 0
    )
    got_frames = from_partner(frame_of_slot, "ctx", 0)
    pair_keys = jnp.concatenate([keep_keys, got_keys], axis=0)
    pair_values = jnp.concatenate([keep_values, got_values], axis=0)
    pair_frames = jnp.concatenate([frame_of_slot, got_frames], axis=0)
    lower = parity == 0
    pair_new_keys = jnp.where(
        lower,
        jnp.concatenate([keep_new_keys, got_new_keys], axis=0),
        jnp.concatenate([got_new_keys, keep_new_keys], axis=0),
    )
    pair_new_values = jnp.where(
        lower,
        jnp.concatenate([keep_new_values, got_new_values], axis=0),
        jnp.concatenate([got_new_values, keep_new_values], axis=0),
    )
    pair_start = (position - parity) * new_keys.shape[0]
    split_heads = jnp.transpose(queries.reshape(rows, groups, group, width), (1, 0, 2, 3))
    outgoing = jnp.tile(split_heads, (shards // groups, 1, 1, 1))
    everyone = lax.all_to_all(outgoing, "ctx", split_axis=0, concat_axis=0, tiled=True).reshape(
        shards * rows, group, width
    )
    my_slopes = lax.dynamic_slice_in_dim(slopes, parity * group, group)
    count = rows * shards
    acc, high, total = attend(
        everyone,
        (
            jnp.zeros((count, 1, group, width), jnp.float32),
            jnp.full((count, 1, group), -1e30, jnp.float32),
            jnp.zeros((count, 1, group), jnp.float32),
        ),
        pair_keys,
        pair_values,
        pair_frames,
        pair_new_keys,
        pair_new_values,
        my_slopes,
        pair_start,
        cache_frames,
    )
    acc, high, total = (
        lax.all_to_all(acc, "ctx", split_axis=0, concat_axis=0, tiled=True),
        lax.all_to_all(high, "ctx", split_axis=0, concat_axis=0, tiled=True),
        lax.all_to_all(total, "ctx", split_axis=0, concat_axis=0, tiled=True),
    )
    acc = acc.reshape(shards // groups, groups, rows, group, width)
    high = high.reshape(shards // groups, groups, rows, group)
    total = total.reshape(shards // groups, groups, rows, group)
    merged = jnp.transpose(combine_sources(acc, high, total), (1, 0, 2, 3))
    result = merged.astype(jnp.bfloat16).reshape(rows, local_heads * width)
    return lax.all_gather(result, "head", axis=1, tiled=True)


def on_device(*arrays):
    fresh, local, width = arrays[0].shape
    cached = arrays[1].shape[0]
    frames = arrays[5].shape[0]
    shards, heads = lax.axis_size("ctx"), lax.axis_size("head")
    whole_tiles = fresh % 16 == 0 and cached % 16 == 0 and width % 128 == 0
    pairs = shards % 2 == 0 and shards > 6 and heads % 2 == 0 and arrays[1].shape[1] == 2
    if whole_tiles and pairs and frames == 1 and (local // arrays[1].shape[1]) % PARTS == 0:
        return in_one_kernel(*arrays)
    return in_steps(*arrays)


def solution(mesh):
    return jax.shard_map(
        on_device,
        mesh=mesh,
        in_specs=(
            P("ctx", "head", None),
            P("ctx", "head", None),
            P("ctx", "head", None),
            P("ctx", "head", None),
            P("ctx", "head", None),
            P("ctx"),
            P("head"),
        ),
        out_specs=P("ctx", None),
        check_vma=False,
    )
```

```python
import functools
import math

import jax
import jax.numpy as jnp
from jax import lax
from jax.experimental import pallas as pl
from jax.experimental.pallas import tpu as pltpu
from jax.sharding import PartitionSpec as P

FRAME = 256
FRAME_BITS = FRAME.bit_length() - 1
MESH = pl.DeviceIdType.MESH
LOG2E = 1.0 / math.log(2.0)
PARTS = 4


def iota(shape, dim):
    return lax.broadcasted_iota(jnp.int32, shape, dim)


def kernel(
    sizes,
    q_in,
    ck_in,
    cv_in,
    nk_in,
    nv_in,
    frame_in,
    slope_in,
    o_ref,
    q_ref,
    ck_ref,
    cv_ref,
    nk_ref,
    nv_ref,
    frame_ref,
    slope_ref,
    kv,
    qb,
    slope_rows,
    acc,
    high,
    total,
    part_out,
    part_in,
    in_sem,
    kv_up,
    kv_down,
    kv_recv,
    q_send,
    q_recv,
    p_send,
    p_recv,
    o_send,
    o_recv,
):
    cached, fresh, groups, group, width, shards, heads = sizes
    column = shards // 2
    rows = group * fresh
    cache_frames = shards
    position = lax.axis_index("ctx")
    me = lax.axis_index("head")
    side = position % 2
    place = position // 2
    across = position + 1 - 2 * side
    sibling = me + 1 - 2 * (me % 2)
    peers = [lax.rem(me + 2 * k, heads) for k in range(1, heads // 2)]
    last = column - 1
    has_up = place < last
    has_down = place > 0
    scale = LOG2E / width**0.5
    k_at = fresh
    f_at = fresh + cached
    v_at = f_at + 16
    n_at = v_at + cached

    fetches = [
        pltpu.make_async_copy(src, dst, in_sem.at[k])
        for k, (src, dst) in enumerate(
            (
                (ck_in, ck_ref),
                (nk_in, nk_ref),
                (cv_in, cv_ref),
                (nv_in, nv_ref),
                (frame_in, frame_ref),
                (q_in, q_ref),
                (slope_in, slope_ref),
            )
        )
    ]
    for fetch in fetches:
        fetch.start()

    barrier = pltpu.get_barrier_semaphore()
    pl.semaphore_signal(barrier, inc=1, device_id={"ctx": across}, device_id_type=MESH)
    for other in [sibling] + peers:
        pl.semaphore_signal(barrier, inc=1, device_id={"head": other}, device_id_type=MESH)

    @pl.when(has_up)
    def _():
        pl.semaphore_signal(barrier, inc=1, device_id={"ctx": position + 2}, device_id_type=MESH)

    @pl.when(has_down)
    def _():
        pl.semaphore_signal(barrier, inc=1, device_id={"ctx": position - 2}, device_id_type=MESH)

    pieces = ((0, v_at), (v_at, n_at + fresh))

    def slab_copy(src, g, h, to_up):
        start, stop = pieces[h]
        if not to_up:
            start, stop = max(start, k_at), min(stop, n_at)
        ref = kv.at[src, g, start:stop]
        return pltpu.make_async_remote_copy(
            src_ref=ref,
            dst_ref=ref,
            send_sem=(kv_up if to_up else kv_down).at[src, g, h],
            recv_sem=kv_recv.at[src, g, h],
            device_id={"ctx": position + 2 if to_up else position - 2},
            device_id_type=MESH,
        )

    def send_own(g, h):
        @pl.when(has_up)
        def _():
            slab_copy(place, g, h, True).start()

        @pl.when(has_down)
        def _():
            slab_copy(place, g, h, False).start()

    slant = iota((cached, groups * cached), 1) - groups * iota((cached, groups * cached), 0)
    picks = [(slant == g).astype(jnp.float32).astype(jnp.bfloat16) for g in range(groups)]
    for fetch in fetches[:5]:
        fetch.wait()
    frame = frame_ref[0].astype(jnp.float32)
    for g in range(groups):
        pick = picks[g]
        few = pick[:fresh, : groups * fresh]
        for src, at, sel, n in (
            (nk_ref, 0, few, fresh),
            (ck_ref, k_at, pick, cached),
            (nv_ref, n_at, few, fresh),
        ):
            kv[place, g, at : at + n, :] = jnp.dot(
                sel, src[...], preferred_element_type=jnp.float32
            ).astype(jnp.bfloat16)
        turned = jnp.dot(pick, cv_ref[...], preferred_element_type=jnp.float32).T
        for at in range(0, cached, width):
            kv[place, g, v_at + at : v_at + at + width, :] = turned[:, at : at + width].astype(
                jnp.bfloat16
            )
        kv[place, g, f_at:v_at, :] = jnp.full((16, width), frame, jnp.float32).astype(jnp.bfloat16)
        if g == 0:
            pl.semaphore_wait(
                barrier, 1 + heads // 2 + jnp.minimum(place, 1) + jnp.minimum(last - place, 1)
            )

        send_own(g, 0)
        if g == 0:
            send_own(g, 1)

    def q_copy(g):
        return pltpu.make_async_remote_copy(
            src_ref=qb.at[0, g],
            dst_ref=qb.at[1, g],
            send_sem=q_send.at[g],
            recv_sem=q_recv.at[g],
            device_id={"ctx": across},
            device_id_type=MESH,
        )

    for fetch in fetches[5:]:
        fetch.wait()
    local = groups * group
    slant = iota((fresh, local * fresh), 1) - local * iota((fresh, local * fresh), 0)
    for g in range(groups):
        pick = jnp.concatenate(
            [
                (slant == g * group + j).astype(jnp.float32).astype(jnp.bfloat16)
                for j in range(group)
            ],
            axis=0,
        )
        ordered = jnp.dot(pick, q_ref[...], preferred_element_type=jnp.float32)
        qb[0, g] = ordered.T.astype(jnp.bfloat16)
        q_copy(g).start()

    token = iota((1, rows), 1)
    for g in range(groups):
        row = jnp.full((1, rows), slope_ref[g * group])
        for j in range(1, group):
            row = jnp.where(token >= j * fresh, slope_ref[g * group + j], row)
        slope_rows[g] = row * LOG2E
    for j in range(group - 1, 0, -1):
        token = jnp.where(token >= j * fresh, token - j * fresh, token)

    def query_position(r):
        owner = position if r == 0 else across
        return owner * fresh + token

    def frame_of(positions):
        return (cache_frames + jnp.right_shift(positions, FRAME_BITS)).astype(jnp.float32)

    for i in range(2 * groups):
        acc[i] = jnp.zeros((width, rows), jnp.float32)
        high[i] = jnp.full((1, rows), -1e30, jnp.float32)
        total[i] = jnp.zeros((1, rows), jnp.float32)

    def attend(src, g, sides, seen, cols=slice(None)):
        keys = kv[src, g, 0 if seen else k_at : f_at, :]
        values = [kv[src, g, at : at + width, :] for at in range(v_at, n_at, width)]
        if seen:
            values.append(kv[src, g, n_at : n_at + fresh, :].T)
        values = jnp.concatenate(values, axis=1)
        key_frame = kv[src, g, f_at:v_at, :].astype(jnp.float32)[0:1, 0:1]
        key_position = iota((fresh, 1), 0) + (2 * src + side) * fresh
        new_frame = frame_of(key_position)
        slope = slope_rows[g, :, cols]
        before = [
            (high[2 * g + r, :, cols], total[2 * g + r, :, cols], acc[2 * g + r, :, cols])
            for r in sides
        ]
        after = []
        for r, (top, sums, out) in zip(sides, before):
            score = jnp.dot(keys, qb[r, g, :, cols], preferred_element_type=jnp.float32) * scale
            here = query_position(r)[:, cols]
            shift = slope * (key_frame - frame_of(here))
            old = score[fresh:] if seen else score
            now = jnp.maximum(top, jnp.max(old, axis=0, keepdims=True) + shift)
            if seen:
                new = score[:fresh] + slope * (new_frame - frame_of(here))
                new = jnp.where(key_position <= here, new, -1e30)
                now = jnp.maximum(now, jnp.max(new, axis=0, keepdims=True))
            corr = jnp.exp2(top - now)
            old = jnp.exp2(old + (shift - now))
            fresh_sum = jnp.sum(old, axis=0, keepdims=True)
            weight = old.astype(jnp.bfloat16)
            if seen:
                new = jnp.exp2(new - now)
                fresh_sum = fresh_sum + jnp.sum(new, axis=0, keepdims=True)
                weight = jnp.concatenate([weight, new.astype(jnp.bfloat16)], axis=0)
            out = out * corr + jnp.dot(values, weight, preferred_element_type=jnp.float32)
            after.append((now, sums * corr + fresh_sum, out))
        for r, (now, sums, out) in zip(sides, after):
            high[2 * g + r, :, cols] = now
            total[2 * g + r, :, cols] = sums
            acc[2 * g + r, :, cols] = out

    def pass_on(apart, g):
        low = place - apart
        top = place + apart

        @pl.when(low >= 0)
        def _():
            for h in range(2):
                slab_copy(low, g, h, True).wait_recv()

                @pl.when(has_up)
                def _():
                    slab_copy(low, g, h, True).start()

        @pl.when(top <= last)
        def _():
            for h in range(2):
                slab_copy(top, g, h, False).wait_recv()

                @pl.when(has_down)
                def _():
                    slab_copy(top, g, h, False).start()

    def attend_pair(apart, g, sides=(1, 0), cols=slice(None)):
        low = place - apart
        top = place + apart

        @pl.when(low >= 0)
        def _():
            attend(low, g, sides, True, cols)

        @pl.when(top <= last)
        def _():
            attend(top, g, sides, False, cols)

    part_rows = rows // PARTS
    part_heads = group // PARTS

    def p_copy(i):
        return pltpu.make_async_remote_copy(
            src_ref=part_out.at[i],
            dst_ref=part_in.at[i],
            send_sem=p_send.at[i],
            recv_sem=p_recv.at[i],
            device_id={"ctx": across},
            device_id_type=MESH,
        )

    def finish(g, parts=range(PARTS)):
        sub = iota((16, part_rows), 0)
        for c in parts:
            i = g * PARTS + c
            cols = slice(c * part_rows, (c + 1) * part_rows)
            sums = total[2 * g + 1, :, cols]
            part_out[i, 0:width, :] = (acc[2 * g + 1, :, cols] * (1.0 / sums)).astype(jnp.bfloat16)
            lse = high[2 * g + 1, :, cols] + jnp.log(sums) * LOG2E
            one = lse.astype(jnp.bfloat16).astype(jnp.float32)
            two = (lse - one).astype(jnp.bfloat16).astype(jnp.float32)
            three = lse - one - two
            stats = jnp.where(sub == 0, one, jnp.where(sub == 1, two, three))
            part_out[i, width : width + 16, :] = stats.astype(jnp.bfloat16)
            p_copy(i).start()

    def block_of(owner, i):
        at = (owner * groups * PARTS + i) * part_heads * width
        return o_ref.at[:, pl.ds(pl.multiple_of(at, part_heads * width), part_heads * width)]

    def o_copy(owner, i, slot, target):
        return pltpu.make_async_remote_copy(
            src_ref=block_of(owner, i),
            dst_ref=block_of(owner, i),
            send_sem=o_send.at[slot, i],
            recv_sem=o_recv.at[owner, i],
            device_id={"head": target},
            device_id_type=MESH,
        )

    def combine(i):
        g, c = divmod(i, PARTS)
        cols = slice(c * part_rows, (c + 1) * part_rows)
        sums = total[2 * g, :, cols]
        mine = high[2 * g, :, cols] + jnp.log(sums) * LOG2E
        p_copy(i).wait_recv()
        stats = part_in[i, width : width + 16, :].astype(jnp.float32)
        theirs = stats[0:1] + stats[1:2] + stats[2:3]
        top = jnp.maximum(mine, theirs)
        a = jnp.exp2(mine - top)
        b = jnp.exp2(theirs - top)
        both = a + b
        out = acc[2 * g, :, cols] * (a / (sums * both)) + part_in[i, 0:width, :].astype(
            jnp.float32
        ) * (b / both)
        out = out.T
        at = (me * groups * PARTS + i) * part_heads * width
        for j in range(part_heads):
            spot = pl.multiple_of(at + j * width, width)
            o_ref[:, pl.ds(spot, width)] = out[j * fresh : (j + 1) * fresh].astype(jnp.bfloat16)
        for k, peer in enumerate(peers):
            o_copy(me, i, 1 + k, peer).start()
        o_copy(me, i, 0, sibling).start()

    def forward(i):
        for k, peer in enumerate(peers):
            o_copy(peer, i, 0, sibling).wait_recv()
            o_copy(peer, i, 1 + len(peers) + k, sibling).start()

    def body(k, carry):
        g = jnp.where(k == 0, 0, 1 - k % 2)
        apart = jnp.where(k == 0, 1, jnp.where(k % 2 == 1, (k + 3) // 2, k // 2))
        pass_on(apart, g)

        @pl.when(k == 0)
        def _():
            send_own(1, 1)

        @pl.when(apart == 1)
        def _():
            q_copy(g).wait_recv()
            attend(place, g, (1,), True)

        attend_pair(apart, g)
        return carry

    count = groups * PARTS
    for g in range(groups):
        attend(place, g, (0,), True)
    lax.fori_loop(0, 2 * last - 3, body, 0)
    pass_on(last, 0)
    attend_pair(last, 0, (1,))
    finish(0)
    attend_pair(last, 0, (0,))
    pass_on(last - 1, 1)
    attend_pair(last - 1, 1)
    for c in range(PARTS):
        combine(c)
    pass_on(last, 1)
    half = PARTS // 2
    for c in (0, half):
        attend_pair(last, 1, (1,), slice(c * part_rows, (c + half) * part_rows))
        finish(1, range(c, c + half))
    attend_pair(last, 1, (0,))
    for c in range(PARTS):
        combine(count - PARTS + c)
        for g in range(groups - 1):
            forward(g * PARTS + c)
    for i in range(count - PARTS, count):
        forward(i)
    for i in range(count):
        o_copy(sibling, i, 0, sibling).wait_recv()
        for peer in peers:
            far = peer + 1 - 2 * (peer % 2)
            o_copy(far, i, 0, sibling).wait_recv()

    for g in range(groups):
        for src in range(column):

            @pl.when(jnp.logical_and(has_up, src <= place))
            def _():
                for h in range(2):
                    slab_copy(src, g, h, True).wait_send()

            @pl.when(jnp.logical_and(has_down, src >= place))
            def _():
                for h in range(2):
                    slab_copy(src, g, h, False).wait_send()

        q_copy(g).wait_send()
    for i in range(count):
        p_copy(i).wait_send()
        o_copy(me, i, 0, sibling).wait_send()
        for k, peer in enumerate(peers):
            o_copy(me, i, 1 + k, peer).wait_send()
            o_copy(peer, i, 1 + len(peers) + k, sibling).wait_send()


def in_one_kernel(queries, cache_keys, cache_values, new_keys, new_values, frame_of_slot, slopes):
    fresh, local, width = queries.shape
    cached, groups, _ = cache_keys.shape
    group = local // groups
    shards = lax.axis_size("ctx")
    heads = lax.axis_size("head")
    column = shards // 2
    rows = group * fresh
    slab = 2 * (cached + fresh) + 16
    count = groups * PARTS
    vmem = pl.BlockSpec(memory_space=pltpu.VMEM)
    dma = pltpu.SemaphoreType.DMA
    sizes = (cached, fresh, groups, group, width, shards, heads)
    return pl.pallas_call(
        functools.partial(kernel, sizes),
        out_shape=pltpu.VMEM((fresh, heads * local * width), jnp.bfloat16),
        in_specs=[pl.BlockSpec(memory_space=pl.ANY)] * 7,
        out_specs=vmem,
        scratch_shapes=[
            pltpu.VMEM((fresh * local, width), jnp.bfloat16),
            pltpu.VMEM((cached * groups, width), jnp.bfloat16),
            pltpu.VMEM((cached * groups, width), jnp.bfloat16),
            pltpu.VMEM((fresh * groups, width), jnp.bfloat16),
            pltpu.VMEM((fresh * groups, width), jnp.bfloat16),
            pltpu.SMEM(frame_of_slot.shape, jnp.int32),
            pltpu.SMEM(slopes.shape, jnp.float32),
            pltpu.VMEM((column, groups, slab, width), jnp.bfloat16),
            pltpu.VMEM((2, groups, width, rows), jnp.bfloat16),
            pltpu.VMEM((groups, 1, rows), jnp.float32),
            pltpu.VMEM((2 * groups, width, rows), jnp.float32),
            pltpu.VMEM((2 * groups, 1, rows), jnp.float32),
            pltpu.VMEM((2 * groups, 1, rows), jnp.float32),
            pltpu.VMEM((count, width + 16, rows // PARTS), jnp.bfloat16),
            pltpu.VMEM((count, width + 16, rows // PARTS), jnp.bfloat16),
            dma((7,)),
            dma((column, groups, 2)),
            dma((column, groups, 2)),
            dma((column, groups, 2)),
            dma((groups,)),
            dma((groups,)),
            dma((count,)),
            dma((count,)),
            dma((heads - 1, count)),
            dma((heads, count)),
        ],
        compiler_params=pltpu.CompilerParams(
            collective_id=0, has_side_effects=True, vmem_limit_bytes=62 * 1024 * 1024
        ),
        name="attend_over_slice",
    )(
        queries.reshape(fresh * local, width),
        cache_keys.reshape(cached * groups, width),
        cache_values.reshape(cached * groups, width),
        new_keys.reshape(fresh * groups, width),
        new_values.reshape(fresh * groups, width),
        frame_of_slot,
        slopes,
    )


def from_partner(value, axis, apart):
    return lax.ppermute(value, axis, [(i, i ^ 1 << apart) for i in range(lax.axis_size(axis))])


def update(state, score, values):
    acc, high, total = state
    new_high = jnp.maximum(high, jnp.max(score, axis=-1))
    corr = jnp.exp(high - new_high)
    expo = jnp.exp(score - new_high[..., None])
    total = total * corr + jnp.sum(expo, axis=-1)
    weight = expo.astype(jnp.bfloat16)
    acc = acc * corr[..., None] + jnp.einsum(
        "rgqk,kgd->rgqd", weight, values, preferred_element_type=jnp.float32
    )
    return (acc, new_high, total)


def attend(
    q_rows,
    state,
    cache_keys,
    cache_values,
    key_frames,
    new_keys,
    new_values,
    slopes,
    key_start,
    cache_frames,
):
    rows, local_heads, width = q_rows.shape
    groups = cache_keys.shape[1]
    group = local_heads // groups
    scale = 1.0 / width**0.5
    query = q_rows.reshape(rows, groups, group, width)
    qpos = jnp.arange(rows, dtype=jnp.int32)
    qframe = (cache_frames + qpos // FRAME).astype(jnp.float32)
    slope = slopes.reshape(groups, group)
    frames = key_frames.shape[0]
    kblocks = cache_keys.reshape(frames, FRAME, groups, width)
    vblocks = cache_values.reshape(frames, FRAME, groups, width)

    def scan_step(carry, items):
        kb, vb, fb = items
        score = jnp.einsum("rgqd,kgd->rgqk", query, kb, preferred_element_type=jnp.float32) * scale
        distance = qframe - fb.astype(jnp.float32)
        score = score - slope[None, :, :, None] * distance[:, None, None, None]
        return (update(carry, score, vb), None)

    state, _ = lax.scan(scan_step, state, (kblocks, vblocks, key_frames))
    kpos = key_start + jnp.arange(new_keys.shape[0], dtype=jnp.int32)
    kframe = (cache_frames + kpos // FRAME).astype(jnp.float32)
    score = (
        jnp.einsum("rgqd,kgd->rgqk", query, new_keys, preferred_element_type=jnp.float32) * scale
    )
    score = score - slope[None, :, :, None] * (qframe[:, None] - kframe[None, :])[:, None, None, :]
    visible = kpos[None, :] <= qpos[:, None]
    score = jnp.where(visible[:, None, None, :], score, -1e30)
    return update(state, score, new_values)


def combine_sources(acc, high, total):
    top = jnp.max(high, axis=0)
    scaling = jnp.exp(high - top[None])
    return jnp.sum(acc * scaling[..., None], axis=0) / jnp.sum(total * scaling, axis=0)[..., None]


def in_steps(queries, cache_keys, cache_values, new_keys, new_values, frame_of_slot, slopes):
    rows, local_heads, width = queries.shape
    groups = cache_keys.shape[1]
    group = local_heads // groups
    shards = lax.axis_size("ctx")
    position = lax.axis_index("ctx")
    cache_frames = frame_of_slot.shape[0] * shards
    parity = position % 2
    other = 1 - parity
    keep_keys = lax.dynamic_slice_in_dim(cache_keys, parity, 1, 1)
    keep_values = lax.dynamic_slice_in_dim(cache_values, parity, 1, 1)
    keep_new_keys = lax.dynamic_slice_in_dim(new_keys, parity, 1, 1)
    keep_new_values = lax.dynamic_slice_in_dim(new_values, parity, 1, 1)
    sent = (
        lax.dynamic_slice_in_dim(cache_keys, other, 1, 1),
        lax.dynamic_slice_in_dim(cache_values, other, 1, 1),
        lax.dynamic_slice_in_dim(new_keys, other, 1, 1),
        lax.dynamic_slice_in_dim(new_values, other, 1, 1),
    )
    got_keys, got_values, got_new_keys, got_new_values = from_partner(
        (sent[0], sent[1], sent[2], sent[3]), "ctx", 0
    )
    got_frames = from_partner(frame_of_slot, "ctx", 0)
    pair_keys = jnp.concatenate([keep_keys, got_keys], axis=0)
    pair_values = jnp.concatenate([keep_values, got_values], axis=0)
    pair_frames = jnp.concatenate([frame_of_slot, got_frames], axis=0)
    lower = parity == 0
    pair_new_keys = jnp.where(
        lower,
        jnp.concatenate([keep_new_keys, got_new_keys], axis=0),
        jnp.concatenate([got_new_keys, keep_new_keys], axis=0),
    )
    pair_new_values = jnp.where(
        lower,
        jnp.concatenate([keep_new_values, got_new_values], axis=0),
        jnp.concatenate([got_new_values, keep_new_values], axis=0),
    )
    pair_start = (position - parity) * new_keys.shape[0]
    split_heads = jnp.transpose(queries.reshape(rows, groups, group, width), (1, 0, 2, 3))
    outgoing = jnp.tile(split_heads, (shards // groups, 1, 1, 1))
    everyone = lax.all_to_all(outgoing, "ctx", split_axis=0, concat_axis=0, tiled=True).reshape(
        shards * rows, group, width
    )
    my_slopes = lax.dynamic_slice_in_dim(slopes, parity * group, group)
    count = rows * shards
    acc, high, total = attend(
        everyone,
        (
            jnp.zeros((count, 1, group, width), jnp.float32),
            jnp.full((count, 1, group), -1e30, jnp.float32),
            jnp.zeros((count, 1, group), jnp.float32),
        ),
        pair_keys,
        pair_values,
        pair_frames,
        pair_new_keys,
        pair_new_values,
        my_slopes,
        pair_start,
        cache_frames,
    )
    acc, high, total = (
        lax.all_to_all(acc, "ctx", split_axis=0, concat_axis=0, tiled=True),
        lax.all_to_all(high, "ctx", split_axis=0, concat_axis=0, tiled=True),
        lax.all_to_all(total, "ctx", split_axis=0, concat_axis=0, tiled=True),
    )
    acc = acc.reshape(shards // groups, groups, rows, group, width)
    high = high.reshape(shards // groups, groups, rows, group)
    total = total.reshape(shards // groups, groups, rows, group)
    merged = jnp.transpose(combine_sources(acc, high, total), (1, 0, 2, 3))
    result = merged.astype(jnp.bfloat16).reshape(rows, local_heads * width)
    return lax.all_gather(result, "head", axis=1, tiled=True)


def on_device(*arrays):
    fresh, local, width = arrays[0].shape
    cached = arrays[1].shape[0]
    frames = arrays[5].shape[0]
    shards, heads = lax.axis_size("ctx"), lax.axis_size("head")
    whole_tiles = fresh % 16 == 0 and cached % width == 0 and width % 128 == 0
    pairs = shards % 2 == 0 and shards > 6 and heads % 2 == 0 and arrays[1].shape[1] == 2
    if whole_tiles and pairs and frames == 1 and (local // arrays[1].shape[1]) % PARTS == 0:
        return in_one_kernel(*arrays)
    return in_steps(*arrays)


def solution(mesh):
    return jax.shard_map(
        on_device,
        mesh=mesh,
        in_specs=(
            P("ctx", "head", None),
            P("ctx", "head", None),
            P("ctx", "head", None),
            P("ctx", "head", None),
            P("ctx", "head", None),
            P("ctx"),
            P("head"),
        ),
        out_specs=P("ctx", None),
        check_vma=False,
    )
```

```python
import functools
import math

import jax
import jax.numpy as jnp
from jax import lax
from jax.experimental import pallas as pl
from jax.experimental.pallas import tpu as pltpu
from jax.sharding import PartitionSpec as P

FRAME = 256
FRAME_BITS = FRAME.bit_length() - 1
MESH = pl.DeviceIdType.MESH
LOG2E = 1.0 / math.log(2.0)
PARTS = 4


def iota(shape, dim):
    return lax.broadcasted_iota(jnp.int32, shape, dim)


def kernel(
    sizes,
    q_in,
    ck_in,
    cv_in,
    nk_in,
    nv_in,
    frame_in,
    slope_in,
    o_ref,
    q_ref,
    ck_ref,
    cv_ref,
    nk_ref,
    nv_ref,
    frame_ref,
    slope_ref,
    kv,
    qb,
    slope_rows,
    acc,
    high,
    total,
    part_out,
    part_in,
    in_sem,
    kv_up,
    kv_down,
    kv_recv,
    q_send,
    q_recv,
    p_send,
    p_recv,
    o_send,
    o_recv,
):
    cached, fresh, groups, group, width, shards, heads = sizes
    column = shards // 2
    rows = group * fresh
    cache_frames = shards
    position = lax.axis_index("ctx")
    me = lax.axis_index("head")
    side = position % 2
    place = position // 2
    across = position + 1 - 2 * side
    sibling = me + 1 - 2 * (me % 2)
    peers = [lax.rem(me + 2 * k, heads) for k in range(1, heads // 2)]
    last = column - 1
    has_up = place < last
    has_down = place > 0
    scale = LOG2E / width**0.5
    k_at = fresh
    f_at = fresh + cached
    v_at = f_at + 16
    n_at = v_at + cached

    fetches = [
        pltpu.make_async_copy(src, dst, in_sem.at[k])
        for k, (src, dst) in enumerate(
            (
                (ck_in, ck_ref),
                (nk_in, nk_ref),
                (frame_in, frame_ref),
                (cv_in, cv_ref),
                (nv_in, nv_ref),
                (q_in, q_ref),
                (slope_in, slope_ref),
            )
        )
    ]
    for fetch in fetches:
        fetch.start()

    barrier = pltpu.get_barrier_semaphore()
    pl.semaphore_signal(barrier, inc=1, device_id={"ctx": across}, device_id_type=MESH)
    for other in [sibling] + peers:
        pl.semaphore_signal(barrier, inc=1, device_id={"head": other}, device_id_type=MESH)

    @pl.when(has_up)
    def _():
        pl.semaphore_signal(barrier, inc=1, device_id={"ctx": position + 2}, device_id_type=MESH)

    @pl.when(has_down)
    def _():
        pl.semaphore_signal(barrier, inc=1, device_id={"ctx": position - 2}, device_id_type=MESH)

    pieces = ((0, v_at), (v_at, n_at + fresh))

    def slab_copy(src, g, h, to_up):
        start, stop = pieces[h]
        if not to_up:
            start, stop = max(start, k_at), min(stop, n_at)
        ref = kv.at[src, g, start:stop]
        return pltpu.make_async_remote_copy(
            src_ref=ref,
            dst_ref=ref,
            send_sem=(kv_up if to_up else kv_down).at[src, g, h],
            recv_sem=kv_recv.at[src, g, h],
            device_id={"ctx": position + 2 if to_up else position - 2},
            device_id_type=MESH,
        )

    def send_own(g, h):
        @pl.when(has_up)
        def _():
            slab_copy(place, g, h, True).start()

        @pl.when(has_down)
        def _():
            slab_copy(place, g, h, False).start()

    slant = iota((cached, groups * cached), 1) - groups * iota((cached, groups * cached), 0)
    picks = [(slant == g).astype(jnp.float32).astype(jnp.bfloat16) for g in range(groups)]
    for fetch in fetches[:3]:
        fetch.wait()
    frame = frame_ref[0].astype(jnp.float32)
    for g in range(groups):
        pick = picks[g]
        few = pick[:fresh, : groups * fresh]
        for src, at, sel, n in (
            (nk_ref, 0, few, fresh),
            (ck_ref, k_at, pick, cached),
        ):
            kv[place, g, at : at + n, :] = jnp.dot(
                sel, src[...], preferred_element_type=jnp.float32
            ).astype(jnp.bfloat16)
        kv[place, g, f_at:v_at, :] = jnp.full((16, width), frame, jnp.float32).astype(jnp.bfloat16)
        if g == 0:
            pl.semaphore_wait(
                barrier, 1 + heads // 2 + jnp.minimum(place, 1) + jnp.minimum(last - place, 1)
            )

        send_own(g, 0)
        if g == 0:
            for fetch in fetches[3:5]:
                fetch.wait()
        turned = jnp.dot(pick, cv_ref[...], preferred_element_type=jnp.float32).T
        for at in range(0, cached, width):
            kv[place, g, v_at + at : v_at + at + width, :] = turned[:, at : at + width].astype(
                jnp.bfloat16
            )
        kv[place, g, n_at : n_at + fresh, :] = jnp.dot(
            few, nv_ref[...], preferred_element_type=jnp.float32
        ).astype(jnp.bfloat16)
        if g == 0:
            send_own(g, 1)

    def q_copy(g):
        return pltpu.make_async_remote_copy(
            src_ref=qb.at[0, g],
            dst_ref=qb.at[1, g],
            send_sem=q_send.at[g],
            recv_sem=q_recv.at[g],
            device_id={"ctx": across},
            device_id_type=MESH,
        )

    for fetch in fetches[5:]:
        fetch.wait()
    local = groups * group
    slant = iota((fresh, local * fresh), 1) - local * iota((fresh, local * fresh), 0)
    for g in range(groups):
        pick = jnp.concatenate(
            [
                (slant == g * group + j).astype(jnp.float32).astype(jnp.bfloat16)
                for j in range(group)
            ],
            axis=0,
        )
        ordered = jnp.dot(pick, q_ref[...], preferred_element_type=jnp.float32)
        qb[0, g] = ordered.T.astype(jnp.bfloat16)
        q_copy(g).start()

    token = iota((1, rows), 1)
    for g in range(groups):
        row = jnp.full((1, rows), slope_ref[g * group])
        for j in range(1, group):
            row = jnp.where(token >= j * fresh, slope_ref[g * group + j], row)
        slope_rows[g] = row * LOG2E
    for j in range(group - 1, 0, -1):
        token = jnp.where(token >= j * fresh, token - j * fresh, token)

    def query_position(r):
        owner = position if r == 0 else across
        return owner * fresh + token

    def frame_of(positions):
        return (cache_frames + jnp.right_shift(positions, FRAME_BITS)).astype(jnp.float32)

    for i in range(2 * groups):
        acc[i] = jnp.zeros((width, rows), jnp.float32)
        high[i] = jnp.full((1, rows), -1e30, jnp.float32)
        total[i] = jnp.zeros((1, rows), jnp.float32)

    def attend(src, g, sides, seen, cols=slice(None)):
        keys = kv[src, g, 0 if seen else k_at : f_at, :]
        values = [kv[src, g, at : at + width, :] for at in range(v_at, n_at, width)]
        if seen:
            values.append(kv[src, g, n_at : n_at + fresh, :].T)
        values = jnp.concatenate(values, axis=1)
        key_frame = kv[src, g, f_at:v_at, :].astype(jnp.float32)[0:1, 0:1]
        key_position = iota((fresh, 1), 0) + (2 * src + side) * fresh
        new_frame = frame_of(key_position)
        slope = slope_rows[g, :, cols]
        before = [
            (high[2 * g + r, :, cols], total[2 * g + r, :, cols], acc[2 * g + r, :, cols])
            for r in sides
        ]
        after = []
        for r, (top, sums, out) in zip(sides, before):
            score = jnp.dot(keys, qb[r, g, :, cols], preferred_element_type=jnp.float32) * scale
            here = query_position(r)[:, cols]
            shift = slope * (key_frame - frame_of(here))
            old = score[fresh:] if seen else score
            now = jnp.maximum(top, jnp.max(old, axis=0, keepdims=True) + shift)
            if seen:
                new = score[:fresh] + slope * (new_frame - frame_of(here))
                new = jnp.where(key_position <= here, new, -1e30)
                now = jnp.maximum(now, jnp.max(new, axis=0, keepdims=True))
            corr = jnp.exp2(top - now)
            old = jnp.exp2(old + (shift - now))
            fresh_sum = jnp.sum(old, axis=0, keepdims=True)
            weight = old.astype(jnp.bfloat16)
            if seen:
                new = jnp.exp2(new - now)
                fresh_sum = fresh_sum + jnp.sum(new, axis=0, keepdims=True)
                weight = jnp.concatenate([weight, new.astype(jnp.bfloat16)], axis=0)
            out = out * corr + jnp.dot(values, weight, preferred_element_type=jnp.float32)
            after.append((now, sums * corr + fresh_sum, out))
        for r, (now, sums, out) in zip(sides, after):
            high[2 * g + r, :, cols] = now
            total[2 * g + r, :, cols] = sums
            acc[2 * g + r, :, cols] = out

    def pass_on(apart, g):
        low = place - apart
        top = place + apart

        @pl.when(low >= 0)
        def _():
            for h in range(2):
                slab_copy(low, g, h, True).wait_recv()

                @pl.when(has_up)
                def _():
                    slab_copy(low, g, h, True).start()

        @pl.when(top <= last)
        def _():
            for h in range(2):
                slab_copy(top, g, h, False).wait_recv()

                @pl.when(has_down)
                def _():
                    slab_copy(top, g, h, False).start()

    def attend_pair(apart, g, sides=(1, 0), cols=slice(None)):
        low = place - apart
        top = place + apart

        @pl.when(low >= 0)
        def _():
            attend(low, g, sides, True, cols)

        @pl.when(top <= last)
        def _():
            attend(top, g, sides, False, cols)

    part_rows = rows // PARTS
    part_heads = group // PARTS

    def p_copy(i):
        return pltpu.make_async_remote_copy(
            src_ref=part_out.at[i],
            dst_ref=part_in.at[i],
            send_sem=p_send.at[i],
            recv_sem=p_recv.at[i],
            device_id={"ctx": across},
            device_id_type=MESH,
        )

    def finish(g, parts=range(PARTS)):
        sub = iota((16, part_rows), 0)
        for c in parts:
            i = g * PARTS + c
            cols = slice(c * part_rows, (c + 1) * part_rows)
            sums = total[2 * g + 1, :, cols]
            part_out[i, 0:width, :] = (acc[2 * g + 1, :, cols] * (1.0 / sums)).astype(jnp.bfloat16)
            lse = high[2 * g + 1, :, cols] + jnp.log(sums) * LOG2E
            one = lse.astype(jnp.bfloat16).astype(jnp.float32)
            two = (lse - one).astype(jnp.bfloat16).astype(jnp.float32)
            three = lse - one - two
            stats = jnp.where(sub == 0, one, jnp.where(sub == 1, two, three))
            part_out[i, width : width + 16, :] = stats.astype(jnp.bfloat16)
            p_copy(i).start()

    def block_of(owner, i):
        at = (owner * groups * PARTS + i) * part_heads * width
        return o_ref.at[:, pl.ds(pl.multiple_of(at, part_heads * width), part_heads * width)]

    def o_copy(owner, i, slot, target):
        return pltpu.make_async_remote_copy(
            src_ref=block_of(owner, i),
            dst_ref=block_of(owner, i),
            send_sem=o_send.at[slot, i],
            recv_sem=o_recv.at[owner, i],
            device_id={"head": target},
            device_id_type=MESH,
        )

    def combine(i):
        g, c = divmod(i, PARTS)
        cols = slice(c * part_rows, (c + 1) * part_rows)
        sums = total[2 * g, :, cols]
        mine = high[2 * g, :, cols] + jnp.log(sums) * LOG2E
        p_copy(i).wait_recv()
        stats = part_in[i, width : width + 16, :].astype(jnp.float32)
        theirs = stats[0:1] + stats[1:2] + stats[2:3]
        top = jnp.maximum(mine, theirs)
        a = jnp.exp2(mine - top)
        b = jnp.exp2(theirs - top)
        both = a + b
        out = acc[2 * g, :, cols] * (a / (sums * both)) + part_in[i, 0:width, :].astype(
            jnp.float32
        ) * (b / both)
        out = out.T
        at = (me * groups * PARTS + i) * part_heads * width
        for j in range(part_heads):
            spot = pl.multiple_of(at + j * width, width)
            o_ref[:, pl.ds(spot, width)] = out[j * fresh : (j + 1) * fresh].astype(jnp.bfloat16)
        for k, peer in enumerate(peers):
            o_copy(me, i, 1 + k, peer).start()
        o_copy(me, i, 0, sibling).start()

    def forward(i):
        for k, peer in enumerate(peers):
            o_copy(peer, i, 0, sibling).wait_recv()
            o_copy(peer, i, 1 + len(peers) + k, sibling).start()

    def body(k, carry):
        g = jnp.where(k == 0, 0, 1 - k % 2)
        apart = jnp.where(k == 0, 1, jnp.where(k % 2 == 1, (k + 3) // 2, k // 2))
        pass_on(apart, g)

        @pl.when(k == 0)
        def _():
            send_own(1, 1)

        @pl.when(apart == 1)
        def _():
            q_copy(g).wait_recv()
            attend(place, g, (1,), True)

        attend_pair(apart, g)
        return carry

    count = groups * PARTS
    for g in range(groups):
        attend(place, g, (0,), True)
    lax.fori_loop(0, 2 * last - 3, body, 0)
    pass_on(last, 0)
    attend_pair(last, 0, (1,))
    finish(0)
    attend_pair(last, 0, (0,))
    pass_on(last - 1, 1)
    attend_pair(last - 1, 1)
    for c in range(PARTS):
        combine(c)
    pass_on(last, 1)
    half = PARTS // 2
    for c in (0, half):
        attend_pair(last, 1, (1,), slice(c * part_rows, (c + half) * part_rows))
        finish(1, range(c, c + half))
    attend_pair(last, 1, (0,))
    for c in range(PARTS):
        combine(count - PARTS + c)
        for g in range(groups - 1):
            forward(g * PARTS + c)
    for i in range(count - PARTS, count):
        forward(i)
    for i in range(count):
        o_copy(sibling, i, 0, sibling).wait_recv()
        for peer in peers:
            far = peer + 1 - 2 * (peer % 2)
            o_copy(far, i, 0, sibling).wait_recv()

    for g in range(groups):
        for src in range(column):

            @pl.when(jnp.logical_and(has_up, src <= place))
            def _():
                for h in range(2):
                    slab_copy(src, g, h, True).wait_send()

            @pl.when(jnp.logical_and(has_down, src >= place))
            def _():
                for h in range(2):
                    slab_copy(src, g, h, False).wait_send()

        q_copy(g).wait_send()
    for i in range(count):
        p_copy(i).wait_send()
        o_copy(me, i, 0, sibling).wait_send()
        for k, peer in enumerate(peers):
            o_copy(me, i, 1 + k, peer).wait_send()
            o_copy(peer, i, 1 + len(peers) + k, sibling).wait_send()


def in_one_kernel(queries, cache_keys, cache_values, new_keys, new_values, frame_of_slot, slopes):
    fresh, local, width = queries.shape
    cached, groups, _ = cache_keys.shape
    group = local // groups
    shards = lax.axis_size("ctx")
    heads = lax.axis_size("head")
    column = shards // 2
    rows = group * fresh
    slab = 2 * (cached + fresh) + 16
    count = groups * PARTS
    vmem = pl.BlockSpec(memory_space=pltpu.VMEM)
    dma = pltpu.SemaphoreType.DMA
    sizes = (cached, fresh, groups, group, width, shards, heads)
    return pl.pallas_call(
        functools.partial(kernel, sizes),
        out_shape=pltpu.VMEM((fresh, heads * local * width), jnp.bfloat16),
        in_specs=[pl.BlockSpec(memory_space=pl.ANY)] * 7,
        out_specs=vmem,
        scratch_shapes=[
            pltpu.VMEM((fresh * local, width), jnp.bfloat16),
            pltpu.VMEM((cached * groups, width), jnp.bfloat16),
            pltpu.VMEM((cached * groups, width), jnp.bfloat16),
            pltpu.VMEM((fresh * groups, width), jnp.bfloat16),
            pltpu.VMEM((fresh * groups, width), jnp.bfloat16),
            pltpu.SMEM(frame_of_slot.shape, jnp.int32),
            pltpu.SMEM(slopes.shape, jnp.float32),
            pltpu.VMEM((column, groups, slab, width), jnp.bfloat16),
            pltpu.VMEM((2, groups, width, rows), jnp.bfloat16),
            pltpu.VMEM((groups, 1, rows), jnp.float32),
            pltpu.VMEM((2 * groups, width, rows), jnp.float32),
            pltpu.VMEM((2 * groups, 1, rows), jnp.float32),
            pltpu.VMEM((2 * groups, 1, rows), jnp.float32),
            pltpu.VMEM((count, width + 16, rows // PARTS), jnp.bfloat16),
            pltpu.VMEM((count, width + 16, rows // PARTS), jnp.bfloat16),
            dma((7,)),
            dma((column, groups, 2)),
            dma((column, groups, 2)),
            dma((column, groups, 2)),
            dma((groups,)),
            dma((groups,)),
            dma((count,)),
            dma((count,)),
            dma((heads - 1, count)),
            dma((heads, count)),
        ],
        compiler_params=pltpu.CompilerParams(
            collective_id=0, has_side_effects=True, vmem_limit_bytes=62 * 1024 * 1024
        ),
        name="attend_over_slice",
    )(
        queries.reshape(fresh * local, width),
        cache_keys.reshape(cached * groups, width),
        cache_values.reshape(cached * groups, width),
        new_keys.reshape(fresh * groups, width),
        new_values.reshape(fresh * groups, width),
        frame_of_slot,
        slopes,
    )


def from_partner(value, axis, apart):
    return lax.ppermute(value, axis, [(i, i ^ 1 << apart) for i in range(lax.axis_size(axis))])


def update(state, score, values):
    acc, high, total = state
    new_high = jnp.maximum(high, jnp.max(score, axis=-1))
    corr = jnp.exp(high - new_high)
    expo = jnp.exp(score - new_high[..., None])
    total = total * corr + jnp.sum(expo, axis=-1)
    weight = expo.astype(jnp.bfloat16)
    acc = acc * corr[..., None] + jnp.einsum(
        "rgqk,kgd->rgqd", weight, values, preferred_element_type=jnp.float32
    )
    return (acc, new_high, total)


def attend(
    q_rows,
    state,
    cache_keys,
    cache_values,
    key_frames,
    new_keys,
    new_values,
    slopes,
    key_start,
    cache_frames,
):
    rows, local_heads, width = q_rows.shape
    groups = cache_keys.shape[1]
    group = local_heads // groups
    scale = 1.0 / width**0.5
    query = q_rows.reshape(rows, groups, group, width)
    qpos = jnp.arange(rows, dtype=jnp.int32)
    qframe = (cache_frames + qpos // FRAME).astype(jnp.float32)
    slope = slopes.reshape(groups, group)
    frames = key_frames.shape[0]
    kblocks = cache_keys.reshape(frames, FRAME, groups, width)
    vblocks = cache_values.reshape(frames, FRAME, groups, width)

    def scan_step(carry, items):
        kb, vb, fb = items
        score = jnp.einsum("rgqd,kgd->rgqk", query, kb, preferred_element_type=jnp.float32) * scale
        distance = qframe - fb.astype(jnp.float32)
        score = score - slope[None, :, :, None] * distance[:, None, None, None]
        return (update(carry, score, vb), None)

    state, _ = lax.scan(scan_step, state, (kblocks, vblocks, key_frames))
    kpos = key_start + jnp.arange(new_keys.shape[0], dtype=jnp.int32)
    kframe = (cache_frames + kpos // FRAME).astype(jnp.float32)
    score = (
        jnp.einsum("rgqd,kgd->rgqk", query, new_keys, preferred_element_type=jnp.float32) * scale
    )
    score = score - slope[None, :, :, None] * (qframe[:, None] - kframe[None, :])[:, None, None, :]
    visible = kpos[None, :] <= qpos[:, None]
    score = jnp.where(visible[:, None, None, :], score, -1e30)
    return update(state, score, new_values)


def combine_sources(acc, high, total):
    top = jnp.max(high, axis=0)
    scaling = jnp.exp(high - top[None])
    return jnp.sum(acc * scaling[..., None], axis=0) / jnp.sum(total * scaling, axis=0)[..., None]


def in_steps(queries, cache_keys, cache_values, new_keys, new_values, frame_of_slot, slopes):
    rows, local_heads, width = queries.shape
    groups = cache_keys.shape[1]
    group = local_heads // groups
    shards = lax.axis_size("ctx")
    position = lax.axis_index("ctx")
    cache_frames = frame_of_slot.shape[0] * shards
    parity = position % 2
    other = 1 - parity
    keep_keys = lax.dynamic_slice_in_dim(cache_keys, parity, 1, 1)
    keep_values = lax.dynamic_slice_in_dim(cache_values, parity, 1, 1)
    keep_new_keys = lax.dynamic_slice_in_dim(new_keys, parity, 1, 1)
    keep_new_values = lax.dynamic_slice_in_dim(new_values, parity, 1, 1)
    sent = (
        lax.dynamic_slice_in_dim(cache_keys, other, 1, 1),
        lax.dynamic_slice_in_dim(cache_values, other, 1, 1),
        lax.dynamic_slice_in_dim(new_keys, other, 1, 1),
        lax.dynamic_slice_in_dim(new_values, other, 1, 1),
    )
    got_keys, got_values, got_new_keys, got_new_values = from_partner(
        (sent[0], sent[1], sent[2], sent[3]), "ctx", 0
    )
    got_frames = from_partner(frame_of_slot, "ctx", 0)
    pair_keys = jnp.concatenate([keep_keys, got_keys], axis=0)
    pair_values = jnp.concatenate([keep_values, got_values], axis=0)
    pair_frames = jnp.concatenate([frame_of_slot, got_frames], axis=0)
    lower = parity == 0
    pair_new_keys = jnp.where(
        lower,
        jnp.concatenate([keep_new_keys, got_new_keys], axis=0),
        jnp.concatenate([got_new_keys, keep_new_keys], axis=0),
    )
    pair_new_values = jnp.where(
        lower,
        jnp.concatenate([keep_new_values, got_new_values], axis=0),
        jnp.concatenate([got_new_values, keep_new_values], axis=0),
    )
    pair_start = (position - parity) * new_keys.shape[0]
    split_heads = jnp.transpose(queries.reshape(rows, groups, group, width), (1, 0, 2, 3))
    outgoing = jnp.tile(split_heads, (shards // groups, 1, 1, 1))
    everyone = lax.all_to_all(outgoing, "ctx", split_axis=0, concat_axis=0, tiled=True).reshape(
        shards * rows, group, width
    )
    my_slopes = lax.dynamic_slice_in_dim(slopes, parity * group, group)
    count = rows * shards
    acc, high, total = attend(
        everyone,
        (
            jnp.zeros((count, 1, group, width), jnp.float32),
            jnp.full((count, 1, group), -1e30, jnp.float32),
            jnp.zeros((count, 1, group), jnp.float32),
        ),
        pair_keys,
        pair_values,
        pair_frames,
        pair_new_keys,
        pair_new_values,
        my_slopes,
        pair_start,
        cache_frames,
    )
    acc, high, total = (
        lax.all_to_all(acc, "ctx", split_axis=0, concat_axis=0, tiled=True),
        lax.all_to_all(high, "ctx", split_axis=0, concat_axis=0, tiled=True),
        lax.all_to_all(total, "ctx", split_axis=0, concat_axis=0, tiled=True),
    )
    acc = acc.reshape(shards // groups, groups, rows, group, width)
    high = high.reshape(shards // groups, groups, rows, group)
    total = total.reshape(shards // groups, groups, rows, group)
    merged = jnp.transpose(combine_sources(acc, high, total), (1, 0, 2, 3))
    result = merged.astype(jnp.bfloat16).reshape(rows, local_heads * width)
    return lax.all_gather(result, "head", axis=1, tiled=True)


def on_device(*arrays):
    fresh, local, width = arrays[0].shape
    cached = arrays[1].shape[0]
    frames = arrays[5].shape[0]
    shards, heads = lax.axis_size("ctx"), lax.axis_size("head")
    whole_tiles = fresh % 16 == 0 and cached % width == 0 and width % 128 == 0
    pairs = shards % 2 == 0 and shards > 6 and heads % 2 == 0 and arrays[1].shape[1] == 2
    if whole_tiles and pairs and frames == 1 and (local // arrays[1].shape[1]) % PARTS == 0:
        return in_one_kernel(*arrays)
    return in_steps(*arrays)


def solution(mesh):
    return jax.shard_map(
        on_device,
        mesh=mesh,
        in_specs=(
            P("ctx", "head", None),
            P("ctx", "head", None),
            P("ctx", "head", None),
            P("ctx", "head", None),
            P("ctx", "head", None),
            P("ctx"),
            P("head"),
        ),
        out_specs=P("ctx", None),
        check_vma=False,
    )
```
